128 devices in a mesh: lon: 32 (over x, y, z_lo), lat: 4 (over z_hi, core).
Axes of the slice: x: 4, y: 4, z: 4 (z_hi: 2, z_lo: 2; z = z_hi * 2 + z_lo), core: 2. Of those that a mesh axis runs over, the one named last changes fastest.
Arguments:
- features: bfloat16 [256, 4096, 512], P('lat', 'lon'), may hold values from -6 to 6
- head_weight: bfloat16 [512, 76], replicated, may hold values from -0.25 to 0.25
- target: bfloat16 [76, 256, 4096], P(None, 'lat', 'lon'), may hold values from -6 to 6
- metrics: float32 [6, 256, 4096], P(None, 'lat', 'lon'), may hold values from 0.5 to 2
- masks: int32 [4, 256, 4096], P(None, 'lat', 'lon'), may hold values 0 or 1
- partner: int32 [4096], replicated, may hold values from 0 to 4095, as said below
Outputs:
- feature_grad: bfloat16 [256, 4096, 512], P('lat', 'lon')
- weight_grad: float32 [512, 76], P('lon')
The draws below stay inside these ranges and needn't reach their ends.
Inputs may be any that keep to these rules, and one draw needn't show every extreme that they name: partner pairs the columns: partner[partner[i]] = i and partner[i] != i.
All inputs are finite; a program needn't handle non-finite values. No bound on the sum of `masks` on one device may be relied on, other than what follows from the above.
Results may differ from the reference program's by a relative error of at most 0.0049.
Values sent between devices are 32-bit elements; how exact they have to be, the bound alone decides.
A program may use at most 64 MiB of HBM per device.

```python
import math
import jax
import jax.numpy as jnp
from jax import lax

FEAT = 512
LEV = 19
CH = 76
NY = 256
NX = 4096


def draw_partner(key, part):
    key = jax.random.fold_in(key, 7)
    order = jax.random.permutation(key, NX).astype(jnp.int32)
    paired = order.reshape(NX // 2, 2)[:, ::-1].reshape(NX)
    return jnp.zeros((NX,), jnp.int32).at[order].set(paired)


def set_ends(array, stream_key, low, largest):
    place = [jax.random.randint(jax.random.fold_in(stream_key, axis), (), 0, length) for axis, length in enumerate(array.shape)]
    longest = array.shape.index(max(array.shape))
    next_to = place[:longest] + [(place[longest] + 1) % array.shape[longest]] + place[longest + 1:]
    return array.at[tuple(place)].set(low).at[tuple(next_to)].set(largest)


def strengthened(result, stream_key, source, target, shards_of, factor):
    def block_of(axis_at):
        return (jnp.arange(result.shape[axis_at]) // (result.shape[axis_at] // shards_of)).reshape((-1,) + (1,) * (result.ndim - 1 - axis_at))

    near = jax.random.permutation(stream_key, shards_of)[block_of(target)]
    second = (block_of(target) + shards_of // 2) % shards_of
    return jnp.where((block_of(source) == near) | (block_of(source) == second), factor * result, result)


def block_levels(own_key, dims, pieces, smallest, top_value):
    def one(position, shards_of):
        steps = jax.random.uniform(jax.random.fold_in(jax.random.fold_in(own_key, 6), position), (shards_of,), jnp.float32, smallest / len(pieces), top_value / len(pieces))
        return jnp.repeat(jnp.exp(steps), dims[position] // shards_of).reshape((-1,) + (1,) * (len(dims) - position - 1))

    level = one(*pieces[0])
    for cut in pieces[1:]:
        level = level * one(*cut)
    return level


def centred(rng, dims, scale, most, pieces=(), kind=jnp.bfloat16):
    gain = block_levels(rng, dims, pieces, -0.22, 0.18) if pieces else 1.0
    result = jax.random.normal(rng, dims, jnp.float32) * scale * gain
    return jnp.minimum(jnp.maximum(result, -most), most).astype(kind)


def gaussian_with(key, shape, spread, reach, cuts, heavy, held_as=jnp.bfloat16):
    values = spread * jax.random.normal(key, shape, jnp.float32)
    if cuts:
        values = values * block_levels(key, shape, cuts, -0.22, 0.18)
    return jnp.clip(strengthened(values, jax.random.fold_in(key, 3), *heavy), -reach, reach).astype(held_as)


def setup_inputs(seed: int = 0) -> dict:
    arg_keys = jax.random.split(jax.random.key(seed), 7)
    features = gaussian_with(arg_keys[0], (NY, NX, FEAT), 1.0, 6.0, ((0, 4), (1, 32)), (1, 2, 32, 2.75))
    head_weight = centred(arg_keys[1], (FEAT, CH), FEAT ** -0.5, 0.25)
    target = centred(arg_keys[2], (CH, NY, NX), 1.0, 6.0, ((1, 4), (2, 32)))
    metrics = jnp.clip(jnp.exp(math.log(2.0) - 1.3862944 * jax.random.uniform(arg_keys[3], (6, NY, NX), jnp.float32) ** block_levels(arg_keys[3], (6, NY, NX), ((1, 4), (2, 32)), -0.2, 0.2)), 0.5, 2.0)
    masks = set_ends((jax.random.randint(arg_keys[4], (4, NY, NX), 0, 4) < 3).astype(jnp.int32), jax.random.fold_in(arg_keys[4], 1), 0, 1)
    partner = draw_partner(jax.random.fold_in(arg_keys[6], 71), 0)
    return {"features": features, "head_weight": head_weight, "target": target, "metrics": metrics, "masks": masks, "partner": partner}


def reference(features, head_weight, target, metrics, masks, partner):
    cell_rows = features.reshape(NY * NX, FEAT).astype(jnp.float32)
    head_wide = head_weight.astype(jnp.float32)
    predicted = jnp.dot(cell_rows, head_wide, preferred_element_type=jnp.float32, precision=lax.Precision.HIGHEST)
    errors = predicted.T.reshape(4 * LEV, NY, NX) - target.astype(jnp.float32)
    weights = masks.astype(jnp.float32)
    u_err = errors[:LEV] * weights[0]
    v_err = errors[LEV:2 * LEV] * weights[1]
    other = errors[2 * LEV:] * weights[3]
    u_flux = metrics[0] * u_err
    v_flux = metrics[3] * v_err
    u_across = metrics[1] * u_err
    v_across = metrics[2] * v_err
    corner_weight = weights[2] / metrics[4]
    centre_weight = weights[3] / metrics[5]
    v_east = jnp.roll(v_flux, -1, axis=2)
    uy_west = jnp.roll(u_across, 1, axis=2)
    ghost_row = -jnp.take(u_flux[:, NY - 1, :], partner, axis=1)
    u_north = jnp.concatenate([u_flux[:, 1:, :], ghost_row[:, None, :]], 1)
    zero_row = jnp.zeros((LEV, 1, NX), jnp.float32)
    vx_south = jnp.concatenate([zero_row, v_across[:, :-1, :]], 1)
    vorticity = corner_weight * (v_east - v_flux - u_north + u_flux)
    shear = corner_weight * (u_north - u_flux + v_east - v_flux)
    tension = centre_weight * (u_across - uy_west - v_across + vx_south)
    co_vort = weights[2] * vorticity
    co_shear = weights[2] * shear
    co_tension = weights[3] * tension
    summed = co_vort + co_shear
    differ = co_vort - co_shear
    grad_v = jnp.roll(summed, 1, axis=2) - summed
    differ_south = jnp.concatenate([zero_row, differ[:, :-1, :]], 1)
    grad_u = differ - differ_south
    fold_term = jnp.take(differ[:, NY - 1, :], partner, axis=1)
    grad_u = jnp.concatenate([grad_u[:, :-1, :], (grad_u[:, -1, :] + fold_term)[:, None, :]], 1)
    grad_uy = co_tension - jnp.roll(co_tension, -1, axis=2)
    tension_north = jnp.concatenate([co_tension[:, 1:, :], zero_row], 1)
    grad_vx = tension_north - co_tension
    grad_ue = weights[0] * (metrics[0] * grad_u + metrics[1] * grad_uy)
    grad_ve = weights[1] * (metrics[3] * grad_v + metrics[2] * grad_vx)
    grad_other = metrics[5] * other
    grads = jnp.concatenate([grad_ue, grad_ve, grad_other], 0).reshape(4 * LEV, NY * NX).astype(jnp.bfloat16)
    grads_wide = grads.astype(jnp.float32)
    feature_grad = jnp.dot(grads_wide.T, head_wide.T, preferred_element_type=jnp.float32, precision=lax.Precision.HIGHEST).astype(jnp.bfloat16)
    weight_grad = jnp.dot(cell_rows.T, grads_wide.T, preferred_element_type=jnp.float32, precision=lax.Precision.HIGHEST) / (NY * NX)
    return feature_grad.reshape(NY, NX, FEAT), weight_grad
```

```python
import functools

import jax
import jax.numpy as jnp
from jax import lax
from jax.experimental import pallas as pl
from jax.experimental.pallas import tpu as pltpu
from jax.sharding import PartitionSpec as P

LEV = 19
CHP = 96
ROW = 56
MESH = pl.DeviceIdType.MESH
F32 = jnp.float32
BF16 = jnp.bfloat16
NT = (((1,), (1,)), ((), ()))


def lanes(shape):
    return lax.broadcasted_iota(jnp.int32, shape, len(shape) - 1)


def grads_kernel(
    feat, tgt, met, msk, wt, part, gr_out, wp_out, wg_out,
    F, Tb, Tf, M, K, Wv, Pv, Wp, EG, ED, HW, HE, CNW, CSE, CW, FS, FB, GR, ACC, WS, RB, LB,
    fsem, lsem, gsem, hs, hr, fs_s, fs_r, rs_s, rs_r, ls_s, ls_r,
):
    n_lon, n_lat = lax.axis_size("lon"), lax.axis_size("lat")
    lon, lat = lax.axis_index("lon"), lax.axis_index("lat")
    R = tgt.shape[1]
    C = tgt.shape[2]
    ft = feat.shape[1]
    n16 = R // 16
    n8 = R // 8
    cells16 = 16 * C
    cells8 = 8 * C
    blk = ft // n_lon
    top = lat == n_lat - 1
    bottom = lat == 0
    east = lax.rem(lon + 1, n_lon)
    west = lax.rem(lon + n_lon - 1, n_lon)
    up = lax.rem(lat + 1, n_lat)
    down = lax.rem(lat + n_lat - 1, n_lat)

    def fcopy(c):
        at = pl.ds(pl.multiple_of(c * cells16, cells16), cells16)
        return pltpu.make_async_copy(feat.at[at], F.at[at], fsem.at[c])

    small = [
        pltpu.make_async_copy(met, M, lsem.at[0]),
        pltpu.make_async_copy(msk, K, lsem.at[1]),
        pltpu.make_async_copy(wt, Wv, lsem.at[2]),
        pltpu.make_async_copy(part, Pv, lsem.at[3]),
        pltpu.make_async_copy(tgt, Tb, lsem.at[4]),
    ]
    for copy in small:
        copy.start()
    for i in range(n16):
        fcopy((i + n16 - 1) % n16).start()

    @pl.when(bottom)
    def _():
        EG[0:ROW, :] = jnp.zeros((ROW, C), F32)
        CSE[...] = jnp.zeros_like(CSE)

    @pl.when(top)
    def _():
        EG[(R + 1) * ROW : (R + 2) * ROW, :] = jnp.zeros((ROW, C), F32)
        CNW[...] = jnp.zeros_like(CNW)

    barrier = pltpu.get_barrier_semaphore()

    @pl.loop(1, n_lon)
    def _(d):
        pl.semaphore_signal(
            barrier, inc=1, device_id=(lax.rem(lon + d, n_lon), lat), device_id_type=MESH
        )

    for d in range(1, n_lat):
        pl.semaphore_signal(
            barrier, inc=1, device_id=(lon, lax.rem(lat + d, n_lat)), device_id_type=MESH
        )
    pl.semaphore_signal(barrier, inc=1, device_id=(east, down), device_id_type=MESH)
    pl.semaphore_signal(barrier, inc=1, device_id=(west, up), device_id_type=MESH)

    small[0].wait()
    small[1].wait()
    for g in range(n8):
        at = slice(8 * g, 8 * g + 8)
        um, vm = K[0, at, :].astype(F32), K[1, at, :].astype(F32)
        qm, hm = K[2, at, :].astype(F32), K[3, at, :].astype(F32)
        area_h = M[5, at, :]
        qw = 2.0 * qm / M[4, at, :]
        coefs = (
            M[0, at, :] * um, M[1, at, :] * um, M[3, at, :] * vm, M[2, at, :] * vm,
            qw, hm / area_h, area_h * hm, qw,
        )
        for k, value in enumerate(coefs):
            EG[pl.ds((8 * g + 1) * ROW + 24 + k, 8, stride=ROW), :] = value

    small[2].wait()
    p = lax.broadcasted_iota(jnp.int32, (CHP, 4 * LEV), 0)
    c = lax.broadcasted_iota(jnp.int32, (CHP, 4 * LEV), 1)
    pick = ((p < 19) & (c == p)) | ((p >= 24) & (p < 43) & (c == p - 5))
    pick = pick | ((p >= 48) & (p < 86) & (c == p - 10))
    wp = lax.dot_general(
        jnp.where(pick, 1.0, 0.0).astype(BF16), Wv[...], NT, preferred_element_type=F32
    )
    Wp[...] = wp.astype(BF16)
    wp_copy = pltpu.make_async_copy(Wp, wp_out, lsem.at[5])
    wp_copy.start()
    ED[...] = jnp.zeros_like(ED)
    Tf[4 * LEV * R :, :] = jnp.zeros((4 * R, C), F32)
    small[3].wait()
    small[4].wait()

    def send(src, dst, k, device):
        return pltpu.make_async_remote_copy(
            src_ref=src, dst_ref=dst, send_sem=hs.at[k], recv_sem=hr.at[k],
            device_id=device, device_id_type=MESH,
        )

    south_row = EG.at[0:ROW]
    first_row = EG.at[ROW : 2 * ROW]
    last_row = EG.at[R * ROW : (R + 1) * ROW]
    north_row = EG.at[(R + 1) * ROW : (R + 2) * ROW]
    to_north = send(last_row, south_row, 0, (lon, up))
    to_south = send(first_row, north_row, 1, (lon, down))
    to_east = send(ED, HW, 2, (east, lat))
    to_west = send(ED, HE, 3, (west, lat))
    to_nw = send(EG.at[R * ROW + 24 : (R + 1) * ROW], CSE, 4, (west, up))
    to_se = send(EG.at[ROW : ROW + 32], CNW, 5, (east, down))

    def fold_copy(peer, d, slot):
        return pltpu.make_async_remote_copy(
            src_ref=FS, dst_ref=FB.at[slot], send_sem=fs_s.at[d], recv_sem=fs_r.at[slot],
            device_id=(peer, lat), device_id_type=MESH,
        )

    def errors_chunk(i, _):
        chunk = lax.rem(i + n16 - 1, n16)
        r0 = pl.multiple_of(chunk * 16, 16)
        fcopy(chunk).wait()
        for ch in range(4 * LEV):
            at = pl.ds(pl.multiple_of(ch * R + r0, 16), 16)
            Tf[at, :] = Tb[ch, pl.ds(r0, 16), :].astype(F32)
        half = lanes((ROW, C)) >> 1
        packed = ED[...]
        for j4 in range(4):
            cells = pl.ds(pl.multiple_of(chunk * cells16 + j4 * 4 * C, 4 * C), 4 * C)
            predicted = lax.dot_general(Wp[...], F[cells, :], NT, preferred_element_type=F32)
            for j in range(4):
                r = r0 + 4 * j4 + j
                base = pl.multiple_of((r + 1) * ROW, 8)
                mine = predicted[:, j * C : (j + 1) * C]

                def true_at(first, count):
                    return jnp.concatenate(
                        [Tf[pl.ds((first + 8 * k) * R + r, 8, stride=R), :] for k in range(count)], 0
                    )

                EG[pl.ds(base, 24), :] = mine[0:24] - true_at(0, 3)
                EG[pl.ds(base + 32, 24), :] = mine[24:48] - true_at(LEV, 3)
                other = (mine[48:88] - true_at(2 * LEV, 5)) * EG[pl.ds(base + 30, 1), :]
                other = jnp.concatenate([other, jnp.zeros((8, C), F32)], 0)
                q = 4 * j4 + j
                GR[2 * chunk + q // 8, 48:CHP, (q % 8) * C : (q % 8 + 1) * C] = other.astype(BF16)
                packed = jnp.where(
                    half == r, pltpu.roll(EG[pl.ds(base, ROW), :], 2 * r + 1, 1), packed
                )
        ED[...] = packed

        @pl.when(i == 0)
        def _():
            pl.semaphore_wait(barrier, n_lon + n_lat)

            @pl.when(jnp.logical_not(top))
            def _():
                to_north.start()
                to_nw.start()

            @pl.when(top)
            def _():
                row = R * ROW
                flux = EG[row : row + 24, :] * EG[row + 24 : row + 25, :]
                sub = lax.broadcasted_iota(jnp.int32, (24, C), 0)
                FS[...] = jnp.where(sub == 23, EG[row + 28 : row + 29, :], flux)

                @pl.loop(1, n_lon)
                def _(d):
                    fold_copy(lax.rem(lon + d, n_lon), d, lon).start()

                FB[lon] = FS[...]

        @pl.when(i == 1)
        def _():
            @pl.when(jnp.logical_not(bottom))
            def _():
                to_south.start()
                to_se.start()

        return 0

    lax.fori_loop(0, n16, errors_chunk, 0)
    to_east.start()
    to_west.start()

    @pl.when(jnp.logical_not(bottom))
    def _():
        to_north.wait_recv()
        to_nw.wait_recv()

    to_east.wait_recv()
    to_west.wait_recv()

    wide = (24, C)
    lane = lanes(wide)
    even = (lane & 1) == 0

    def roll(x, by):
        return pltpu.roll(x, by, 1)

    he = roll(HE[...], C - 1)
    hw = roll(HW[...], 1)
    ed = ED[...]
    flux_e = he[32:56] * he[26:27]
    across_e = he[32:56] * he[27:28]
    corner = CSE[8:32, :] * CSE[3:4, :]
    before = jnp.where(lane == 0, corner, roll(across_e, 2))
    tension_e = he[29:30] * (he[0:24] * he[25:26] - ed[0:24] * ed[25:26] - across_e + before)
    across_w = hw[0:24] * hw[25:26]
    summed_w = hw[28:29] * (ed[32:56] * ed[26:27] - hw[32:56] * hw[26:27])
    edge_a = jnp.where(even, flux_e, across_w)
    edge_b = jnp.where(even, tension_e, summed_w)

    def u_at(base):
        return EG[pl.ds(base, 24), :]

    def v_at(base):
        return EG[pl.ds(base + 32, 24), :]

    def coef(base, k):
        return EG[pl.ds(base + 24 + k, 1), :]

    def shifted_west(x, edge):
        return jnp.where(lane == 0, edge, roll(x, 1))

    def shifted_east(x, edge):
        return jnp.where(lane == C - 1, edge, roll(x, C - 1))

    uf0 = u_at(ROW) * coef(ROW, 0)
    va0 = v_at(ROW) * coef(ROW, 3)
    ra0 = roll(edge_a, C - 1)
    ua0 = u_at(ROW) * coef(ROW, 1)
    ct0 = coef(ROW, 5) * (ua0 - shifted_west(ua0, ra0) - va0 + v_at(0) * coef(0, 3))
    df0 = coef(0, 7) * (u_at(0) * coef(0, 0) - uf0)

    ACC[...] = jnp.zeros_like(ACC)
    CW[...] = jnp.zeros_like(CW)

    def stencil_chunk(i, carry):
        uf, va, ct, df, ra = carry
        last = i == n8 - 1

        @pl.when(last)
        def _():
            @pl.when(jnp.logical_not(top))
            def _():
                to_south.wait_recv()
                to_se.wait_recv()

            CW[...] = roll(CNW[0:24, :] * CNW[25:26, :], 1)

            @pl.when(top)
            def _():
                @pl.loop(1, n_lon)
                def _(d):
                    slot = lax.rem(lon + n_lon - d, n_lon)
                    fold_copy(slot, d, slot).wait_recv()

                mirror = Pv[pl.ds(lon, 1), :]
                which = jnp.broadcast_to(mirror >> 7, wide)
                within = jnp.broadcast_to(mirror & 127, wide)

                def look(b, found):
                    there = jnp.take_along_axis(FB[b], within, axis=1, mode="promise_in_bounds")
                    return jnp.where(which == b, there, found)

                found = lax.fori_loop(0, n_lon, look, jnp.zeros(wide, F32))
                beyond = (R + 1) * ROW
                EG[beyond : beyond + 24, :] = -found
                EG[beyond + 24 : beyond + 25, :] = jnp.ones((1, C), F32)
                at = R * ROW + 31
                EG[at : at + 1, :] = EG[at : at + 1, :] + found[23:24]

        for j in range(8):
            r = 8 * i + j
            b0 = pl.multiple_of((r + 1) * ROW, 8)
            b1 = pl.multiple_of((r + 2) * ROW, 8)
            u1, v1 = u_at(b1), v_at(b1)
            uf1, ua1, va1 = u1 * coef(b1, 0), u1 * coef(b1, 1), v1 * coef(b1, 3)
            ra1 = roll(edge_a, lax.rem(4 * C - 3 - 2 * r, C))
            if j == 7:
                ra1 = jnp.where(last, CW[...], ra1)
            rb = roll(edge_b, C - 1 - 2 * r)
            df1 = coef(b0, 7) * (uf - uf1)
            ct1 = coef(b1, 5) * (ua1 - shifted_west(ua1, ra1) - va1 + va)
            vf = v_at(b0) * coef(b0, 2)
            summed = coef(b0, 4) * (shifted_east(vf, ra) - vf)
            grad_v = shifted_west(summed, rb) - summed
            grad_uy = ct - shifted_east(ct, rb)
            gu = coef(b0, 0) * (df1 - df) + coef(b0, 1) * grad_uy
            gv = coef(b0, 2) * grad_v + coef(b0, 3) * (ct1 - ct)
            GR[i, 0:48, j * C : (j + 1) * C] = jnp.concatenate([gu, gv], 0).astype(BF16)
            uf, va, ct, df, ra = uf1, va1, ct1, df1, ra1
        pltpu.make_async_copy(GR.at[i], gr_out.at[i], gsem.at[i]).start()
        cells = pl.ds(pl.multiple_of(i * cells8, cells8), cells8)
        ACC[...] += jnp.dot(GR[i], F[cells, :], preferred_element_type=F32)
        return uf, va, ct, df, ra

    lax.fori_loop(0, n8, stencil_chunk, (uf0, va0, ct0, df0, ra0))

    scale = 1.0 / (R * n_lat * C * n_lon)
    acc = ACC[...] * scale
    acc = jnp.concatenate([acc, jnp.zeros((C - CHP, ft), F32)], 0)
    WS[...] = acc.T

    def rows_copy(peer, d, slot):
        src = WS.at[pl.ds(pl.multiple_of(peer * blk, blk), blk)]
        return pltpu.make_async_remote_copy(
            src_ref=src, dst_ref=RB.at[slot], send_sem=rs_s.at[d], recv_sem=rs_r.at[slot],
            device_id=(peer, lat), device_id_type=MESH,
        )

    @pl.loop(1, n_lon)
    def _(d):
        rows_copy(lax.rem(lon + d, n_lon), d, lon).start()

    RB[lon] = WS[pl.ds(pl.multiple_of(lon * blk, blk), blk), :]

    @pl.loop(1, n_lon)
    def _(d):
        slot = lax.rem(lon + n_lon - d, n_lon)
        rows_copy(slot, d, slot).wait_recv()

    total = RB[0]
    for k in range(1, n_lon):
        total = total + RB[k]
    LB[lat] = total

    def lat_copy(d):
        return pltpu.make_async_remote_copy(
            src_ref=LB.at[lat], dst_ref=LB.at[lat], send_sem=ls_s.at[d], recv_sem=ls_r.at[d],
            device_id=(lon, lax.rem(lat + d, n_lat)), device_id_type=MESH,
        )

    for d in range(1, n_lat):
        lat_copy(d).start()
    for d in range(1, n_lat):
        lat_copy(d).wait_recv()
    total = LB[0]
    for k in range(1, n_lat):
        total = total + LB[k]
    wg_out[...] = total

    for d in range(1, n_lat):
        lat_copy(d).wait_send()

    @pl.loop(1, n_lon)
    def _(d):
        rows_copy(lax.rem(lon + d, n_lon), d, lon).wait_send()

    @pl.when(jnp.logical_not(top))
    def _():
        to_north.wait_send()
        to_nw.wait_send()

    @pl.when(top)
    def _():
        @pl.loop(1, n_lon)
        def _(d):
            fold_copy(lax.rem(lon + d, n_lon), d, lon).wait_send()

    @pl.when(jnp.logical_not(bottom))
    def _():
        to_south.wait_send()
        to_se.wait_send()

    to_east.wait_send()
    to_west.wait_send()
    wp_copy.wait()

    @pl.loop(0, n8)
    def _(i):
        pltpu.make_async_copy(GR.at[i], gr_out.at[i], gsem.at[i]).wait()


def feature_kernel(gr, wp, out):
    out[...] = lax.dot_general(
        gr[0], wp[...], (((0,), (0,)), ((), ())), preferred_element_type=F32
    ).astype(BF16)


def per_device(n_lon, n_lat, features, head_weight, target, metrics, masks, partner):
    R, C, ft = features.shape
    ch = target.shape[0]
    blk = ft // n_lon
    n8 = R // 8
    cells = R * C
    hbm = pl.BlockSpec(memory_space=pl.ANY)
    vmem = pl.BlockSpec(memory_space=pltpu.VMEM)
    V = pltpu.VMEM
    D = pltpu.SemaphoreType.DMA
    gr, wp, wg = pl.pallas_call(
        grads_kernel,
        out_shape=(
            jax.ShapeDtypeStruct((n8, CHP, 8 * C), BF16),
            jax.ShapeDtypeStruct((CHP, ft), BF16),
            jax.ShapeDtypeStruct((blk, C), F32),
        ),
        in_specs=[hbm] * 6,
        out_specs=(hbm, hbm, vmem),
        scratch_shapes=[
            V((cells, ft), BF16),
            V((ch, R, C), BF16),
            V(((ch + 4) * R, C), F32),
            V((6, R, C), F32),
            V((4, R, C), jnp.int32),
            V((ft, ch), BF16),
            V((n_lon, C), jnp.int32),
            V((CHP, ft), BF16),
            V(((R + 2) * ROW, C), F32),
            V((ROW, C), F32),
            V((ROW, C), F32),
            V((ROW, C), F32),
            V((32, C), F32),
            V((32, C), F32),
            V((24, C), F32),
            V((24, C), F32),
            V((n_lon, 24, C), F32),
            V((n8, CHP, 8 * C), BF16),
            V((CHP, ft), F32),
            V((ft, C), F32),
            V((n_lon, blk, C), F32),
            V((n_lat, blk, C), F32),
            D((R // 16,)), D((6,)), D((n8,)), D((6,)), D((6,)),
            D((n_lon,)), D((n_lon,)), D((n_lon,)), D((n_lon,)), D((n_lat,)), D((n_lat,)),
        ],
        compiler_params=pltpu.CompilerParams(
            collective_id=0, has_side_effects=True, vmem_limit_bytes=48 * 1024 * 1024
        ),
        cost_estimate=pl.CostEstimate(
            flops=4 * cells * ft * CHP, bytes_accessed=12 * 1024 * 1024, transcendentals=0
        ),
        name="grads_and_weight_grad",
    )(
        features.reshape(cells, ft), target, metrics, masks, head_weight,
        partner.reshape(n_lon, C),
    )
    feature_grad = pl.pallas_call(
        feature_kernel,
        grid=(n8,),
        out_shape=jax.ShapeDtypeStruct((cells, ft), BF16),
        in_specs=[
            pl.BlockSpec((1, CHP, 8 * C), lambda i: (i, 0, 0)),
            pl.BlockSpec((CHP, ft), lambda i: (0, 0)),
        ],
        out_specs=pl.BlockSpec((8 * C, ft), lambda i: (i, 0)),
        compiler_params=pltpu.CompilerParams(vmem_limit_bytes=32 * 1024 * 1024),
        cost_estimate=pl.CostEstimate(
            flops=2 * cells * ft * CHP, bytes_accessed=10 * 1024 * 1024, transcendentals=0
        ),
        name="feature_grad",
    )(gr, wp)
    weight_grad = jnp.concatenate([wg[:, 0:19], wg[:, 24:43], wg[:, 48:86]], axis=1)
    return feature_grad.reshape(R, C, ft), weight_grad


def solution(mesh):
    return jax.shard_map(
        functools.partial(per_device, mesh.shape["lon"], mesh.shape["lat"]),
        mesh=mesh,
        in_specs=(
            P("lat", "lon", None),
            P(),
            P(None, "lat", "lon"),
            P(None, "lat", "lon"),
            P(None, "lat", "lon"),
            P(),
        ),
        out_specs=(P("lat", "lon", None), P("lon", None)),
        check_vma=False,
    )
```

```python
import functools

import jax
import jax.numpy as jnp
from jax import lax
from jax.experimental import pallas as pl
from jax.experimental.pallas import tpu as pltpu
from jax.sharding import PartitionSpec as P

LEV = 19
CHP = 96
ROW = 56
MESH = pl.DeviceIdType.MESH
F32 = jnp.float32
BF16 = jnp.bfloat16
NT = (((1,), (1,)), ((), ()))
NN = (((1,), (0,)), ((), ()))


def lanes(shape):
    return lax.broadcasted_iota(jnp.int32, shape, len(shape) - 1)


def grads_kernel(
    feat, tgt, met, msk, wt, part, gr_out, wp_out, wg_out,
    F, Tb, Tf, M, K, Wv, Pv, Wp, EG, ED, FE, HW, HE, CNW, CSE, CW, FS, FB, GR, ACC, WS, RB, LB,
    fsem, esem, lsem, gsem, hs, hr, fs_s, fs_r, rs_s, rs_r, ls_s, ls_r,
):
    n_lon, n_lat = lax.axis_size("lon"), lax.axis_size("lat")
    lon, lat = lax.axis_index("lon"), lax.axis_index("lat")
    R, C, ft = feat.shape
    n16 = R // 16
    n8 = R // 8
    blk = ft // n_lon
    top = lat == n_lat - 1
    bottom = lat == 0
    east = lax.rem(lon + 1, n_lon)
    west = lax.rem(lon + n_lon - 1, n_lon)
    up = lax.rem(lat + 1, n_lat)
    down = lax.rem(lat + n_lat - 1, n_lat)

    barrier = pltpu.get_barrier_semaphore()
    pl.semaphore_signal(barrier, inc=1, device_id=(east, lat), device_id_type=MESH)
    pl.semaphore_signal(barrier, inc=1, device_id=(west, lat), device_id_type=MESH)
    for d in range(1, n_lat):
        pl.semaphore_signal(
            barrier, inc=1, device_id=(lon, lax.rem(lat + d, n_lat)), device_id_type=MESH
        )
    pl.semaphore_signal(barrier, inc=1, device_id=(east, down), device_id_type=MESH)
    pl.semaphore_signal(barrier, inc=1, device_id=(west, up), device_id_type=MESH)

    def fcopy(c):
        at = (pl.ds(pl.multiple_of(c * 16, 16), 16), pl.ds(16, C - 32))
        return pltpu.make_async_copy(feat.at[at], F.at[at], fsem.at[c])

    def ecopy(k):
        at = (pl.ds(0, R), pl.ds(k * (C - 16), 16))
        return pltpu.make_async_copy(feat.at[at], F.at[at], esem.at[k])

    small = [
        pltpu.make_async_copy(met, M, lsem.at[0]),
        pltpu.make_async_copy(msk, K, lsem.at[1]),
        pltpu.make_async_copy(wt, Wv, lsem.at[2]),
        pltpu.make_async_copy(part, Pv, lsem.at[3]),
        pltpu.make_async_copy(tgt, Tb, lsem.at[4]),
    ]
    for copy in small:
        copy.start()
    ecopy(0).start()
    ecopy(1).start()
    for i in range(n16):
        fcopy((i + n16 - 1) % n16).start()

    @pl.when(bottom)
    def _():
        EG[0:ROW, :] = jnp.zeros((ROW, C), F32)
        CSE[...] = jnp.zeros_like(CSE)

    @pl.when(top)
    def _():
        EG[(R + 1) * ROW : (R + 2) * ROW, :] = jnp.zeros((ROW, C), F32)
        CNW[...] = jnp.zeros_like(CNW)

    @pl.loop(2, n_lon - 1)
    def _(d):
        pl.semaphore_signal(
            barrier, inc=1, device_id=(lax.rem(lon + d, n_lon), lat), device_id_type=MESH
        )

    small[0].wait()
    small[1].wait()
    for g in range(n8):
        at = slice(8 * g, 8 * g + 8)
        um, vm = K[0, at, :].astype(F32), K[1, at, :].astype(F32)
        qm, hm = K[2, at, :].astype(F32), K[3, at, :].astype(F32)
        area_h = M[5, at, :]
        qw = 2.0 * qm / M[4, at, :]
        coefs = (
            M[0, at, :] * um, M[1, at, :] * um, M[3, at, :] * vm, M[2, at, :] * vm,
            qw, hm / area_h, area_h * hm, qw,
        )
        for k, value in enumerate(coefs):
            EG[pl.ds((8 * g + 1) * ROW + 24 + k, 8, stride=ROW), :] = value

    small[2].wait()
    p = lax.broadcasted_iota(jnp.int32, (CHP, 4 * LEV), 0)
    c = lax.broadcasted_iota(jnp.int32, (CHP, 4 * LEV), 1)
    level = (p // 16) * 8 + p % 8
    pick = (p < 48) & (level < LEV) & (c == level + LEV * ((p // 8) % 2))
    pick = pick | ((p >= 48) & (c == p - 10))
    wp = lax.dot_general(
        jnp.where(pick, 1.0, 0.0).astype(BF16), Wv[...], NN, preferred_element_type=F32
    )
    Wp[...] = wp.astype(BF16)
    wp_copy = pltpu.make_async_copy(Wp, wp_out, lsem.at[5])
    wp_copy.start()
    Tf[4 * LEV * R :, :] = jnp.zeros((4 * R, C), F32)
    small[3].wait()
    small[4].wait()

    def true_at(first, r):
        return Tf[pl.ds(first * R + r, 8, stride=R), :]

    def widen(i, _):
        at = pl.multiple_of(16 * i, 16)
        for ch in range(4 * LEV):
            Tf[pl.ds(pl.multiple_of(ch * R + at, 16), 16), :] = Tb[ch, pl.ds(at, 16), :].astype(F32)
        return 0

    lax.fori_loop(0, n16, widen, 0)

    half = lanes((8, C)) >> 1

    def pack(i, packed):
        packed = list(packed)
        for j in range(16):
            r = 16 * i + j
            base = pl.multiple_of((r + 1) * ROW, 8)
            rows = [true_at(8 * k, r) for k in range(3)]
            rows.append(EG[pl.ds(base + 24, 8), :])
            rows += [true_at(LEV + 8 * k, r) for k in range(3)]
            by = 2 * r + 1
            packed = [
                jnp.where(half == r, pltpu.roll(x, by, 1), y) for x, y in zip(rows, packed)
            ]
        return tuple(packed)

    zero8 = jnp.zeros((8, C), F32)
    packed = lax.fori_loop(0, n16, pack, (zero8,) * 7)
    q = lax.broadcasted_iota(jnp.int32, (32, 512), 0)
    cell = lax.broadcasted_iota(jnp.int32, (32, 512), 1)
    row16 = (q >> 1) * 16
    wanted = row16 + jnp.where((q & 1) == 1, 0, 256 + 15)
    choose = jnp.where(cell == wanted, 1.0, 0.0).astype(BF16)
    ecopy(0).wait()
    ecopy(1).wait()
    for i in range(n16):
        rows = slice(16 * i, 16 * i + 16)
        both = jnp.concatenate(
            [F[rows, 0:16, :].reshape(256, ft), F[rows, C - 16 : C, :].reshape(256, ft)], 0
        )
        FE[32 * i : 32 * i + 32, :] = jnp.dot(
            choose, both, preferred_element_type=F32
        ).astype(BF16)
    at_edges = lax.dot_general(Wp[0:48, :], FE[...], NT, preferred_element_type=F32)
    for k in range(3):
        ED[8 * k : 8 * k + 8, 0 : 2 * R] = (
            at_edges[16 * k : 16 * k + 8] - packed[k][:, 0 : 2 * R]
        )
        ED[32 + 8 * k : 40 + 8 * k, 0 : 2 * R] = (
            at_edges[16 * k + 8 : 16 * k + 16] - packed[4 + k][:, 0 : 2 * R]
        )
    ED[24:32, :] = packed[3]

    def send(src, dst, k, device):
        return pltpu.make_async_remote_copy(
            src_ref=src, dst_ref=dst, send_sem=hs.at[k], recv_sem=hr.at[k],
            device_id=device, device_id_type=MESH,
        )

    south_row = EG.at[0:ROW]
    first_row = EG.at[ROW : 2 * ROW]
    last_row = EG.at[R * ROW : (R + 1) * ROW]
    north_row = EG.at[(R + 1) * ROW : (R + 2) * ROW]
    to_north = send(last_row, south_row, 0, (lon, up))
    to_south = send(first_row, north_row, 1, (lon, down))
    to_east = send(ED, HW, 2, (east, lat))
    to_west = send(ED, HE, 3, (west, lat))
    to_nw = send(EG.at[R * ROW + 24 : (R + 1) * ROW], CSE, 4, (west, up))
    to_se = send(EG.at[ROW : ROW + 32], CNW, 5, (east, down))

    def fold_copy(peer, d, slot):
        return pltpu.make_async_remote_copy(
            src_ref=FS, dst_ref=FB.at[slot], send_sem=fs_s.at[d], recv_sem=fs_r.at[slot],
            device_id=(peer, lat), device_id_type=MESH,
        )

    def errors_chunk(i, _):
        chunk = lax.rem(i + n16 - 1, n16)
        r0 = pl.multiple_of(chunk * 16, 16)
        fcopy(chunk).wait()
        for j4 in range(4):
            cells = F[pl.ds(r0 + 4 * j4, 4), :, :].reshape(4 * C, ft)
            predicted = lax.dot_general(Wp[...], cells, NT, preferred_element_type=F32)
            for j in range(4):
                q = 4 * j4 + j
                r = r0 + q
                base = pl.multiple_of((r + 1) * ROW, 8)
                mine = predicted[:, j * C : (j + 1) * C]
                for k in range(3):
                    EG[pl.ds(base + 8 * k, 8), :] = mine[16 * k : 16 * k + 8] - true_at(8 * k, r)
                    EG[pl.ds(base + 32 + 8 * k, 8), :] = (
                        mine[16 * k + 8 : 16 * k + 16] - true_at(LEV + 8 * k, r)
                    )
                other = [mine[48 + 8 * k : 56 + 8 * k] - true_at(2 * LEV + 8 * k, r) for k in range(5)]
                other = jnp.concatenate(other, 0) * EG[pl.ds(base + 30, 1), :]
                other = jnp.concatenate([other, jnp.zeros((8, C), F32)], 0)
                GR[2 * chunk + q // 8 + 1, 48:CHP, (q % 8) * C : (q % 8 + 1) * C] = other.astype(BF16)

        @pl.when(i == 0)
        def _():
            pl.semaphore_wait(barrier, n_lon + n_lat)
            to_east.start()
            to_west.start()

            @pl.when(jnp.logical_not(top))
            def _():
                to_north.start()
                to_nw.start()

            @pl.when(top)
            def _():
                row = R * ROW
                flux = EG[row : row + 24, :] * EG[row + 24 : row + 25, :]
                sub = lax.broadcasted_iota(jnp.int32, (24, C), 0)
                FS[...] = jnp.where(sub == 23, EG[row + 28 : row + 29, :], flux)

                @pl.loop(1, n_lon)
                def _(d):
                    fold_copy(lax.rem(lon + d, n_lon), d, lon).start()

                FB[lon] = FS[...]

        @pl.when(i == 1)
        def _():
            @pl.when(jnp.logical_not(bottom))
            def _():
                to_south.start()
                to_se.start()

        return 0

    lax.fori_loop(0, n16, errors_chunk, 0)

    @pl.when(jnp.logical_not(bottom))
    def _():
        to_north.wait_recv()
        to_nw.wait_recv()

    to_east.wait_recv()
    to_west.wait_recv()

    wide = (24, C)
    lane = lanes(wide)
    even = (lane & 1) == 0

    def roll(x, by):
        return pltpu.roll(x, by, 1)

    he = roll(HE[...], C - 1)
    hw = roll(HW[...], 1)
    ed = ED[...]
    flux_e = he[32:56] * he[26:27]
    across_e = he[32:56] * he[27:28]
    corner = CSE[8:32, :] * CSE[3:4, :]
    before = jnp.where(lane == 0, corner, roll(across_e, 2))
    tension_e = he[29:30] * (he[0:24] * he[25:26] - ed[0:24] * ed[25:26] - across_e + before)
    across_w = hw[0:24] * hw[25:26]
    summed_w = hw[28:29] * (ed[32:56] * ed[26:27] - hw[32:56] * hw[26:27])
    edge_a = jnp.where(even, flux_e, across_w)
    edge_b = jnp.where(even, tension_e, summed_w)

    lane8 = lanes((8, C))

    def u_at(base, g):
        return EG[pl.ds(base + 8 * g, 8), :]

    def v_at(base, g):
        return EG[pl.ds(base + 32 + 8 * g, 8), :]

    def coef(base, k):
        return EG[pl.ds(base + 24 + k, 1), :]

    def shifted_west(x, edge):
        return jnp.where(lane8 == 0, edge, roll(x, 1))

    def shifted_east(x, edge):
        return jnp.where(lane8 == C - 1, edge, roll(x, C - 1))

    first = []
    for g in range(3):
        uf0 = u_at(ROW, g) * coef(ROW, 0)
        va0 = v_at(ROW, g) * coef(ROW, 3)
        ra0 = roll(edge_a[8 * g : 8 * g + 8], C - 1)
        ua0 = u_at(ROW, g) * coef(ROW, 1)
        before = v_at(0, g) * coef(0, 3)
        ct0 = coef(ROW, 5) * (ua0 - shifted_west(ua0, ra0) - va0 + before)
        df0 = coef(0, 7) * (u_at(0, g) * coef(0, 0) - uf0)
        first.append((uf0, va0, ct0, df0, ra0))

    ACC[...] = jnp.zeros_like(ACC)
    CW[...] = jnp.zeros_like(CW)

    GR[0] = jnp.zeros(GR.shape[1:], BF16)

    def weight_chunk(slot, chunk):
        cells = F[pl.ds(pl.multiple_of(8 * chunk, 8), 8), :, :].reshape(8 * C, ft)
        ACC[...] += jnp.dot(GR[slot], cells, preferred_element_type=F32)

    def stencil_chunk(i, carry):
        last = i == n8 - 1

        @pl.when(last)
        def _():
            @pl.when(jnp.logical_not(top))
            def _():
                to_south.wait_recv()
                to_se.wait_recv()

            CW[...] = roll(CNW[0:24, :] * CNW[25:26, :], 1)

            @pl.when(top)
            def _():
                @pl.loop(1, n_lon)
                def _(d):
                    slot = lax.rem(lon + n_lon - d, n_lon)
                    fold_copy(slot, d, slot).wait_recv()

                mirror = Pv[pl.ds(lon, 1), :]
                which = jnp.broadcast_to(mirror >> 7, wide)
                within = jnp.broadcast_to(mirror & 127, wide)

                def look(b, found):
                    there = jnp.take_along_axis(FB[b], within, axis=1, mode="promise_in_bounds")
                    return jnp.where(which == b, there, found)

                found = lax.fori_loop(0, n_lon, look, jnp.zeros(wide, F32))
                beyond = (R + 1) * ROW
                EG[beyond : beyond + 24, :] = -found
                EG[beyond + 24 : beyond + 25, :] = jnp.ones((1, C), F32)
                at = R * ROW + 31
                EG[at : at + 1, :] = EG[at : at + 1, :] + found[23:24]

        weight_chunk(i, jnp.maximum(i - 1, 0))
        after = []
        for g in range(3):
            uf, va, ct, df, ra = carry[g]
            mine_a = edge_a[8 * g : 8 * g + 8]
            mine_b = edge_b[8 * g : 8 * g + 8]
            for j in range(8):
                r = 8 * i + j
                b0 = pl.multiple_of((r + 1) * ROW, 8)
                b1 = pl.multiple_of((r + 2) * ROW, 8)
                u1, v1 = u_at(b1, g), v_at(b1, g)
                uf1, ua1, va1 = u1 * coef(b1, 0), u1 * coef(b1, 1), v1 * coef(b1, 3)
                ra1 = roll(mine_a, lax.rem(4 * C - 3 - 2 * r, C))
                if j == 7:
                    ra1 = jnp.where(last, CW[8 * g : 8 * g + 8, :], ra1)
                rb = roll(mine_b, C - 1 - 2 * r)
                df1 = coef(b0, 7) * (uf - uf1)
                ct1 = coef(b1, 5) * (ua1 - shifted_west(ua1, ra1) - va1 + va)
                vf = v_at(b0, g) * coef(b0, 2)
                summed = coef(b0, 4) * (shifted_east(vf, ra) - vf)
                grad_v = shifted_west(summed, rb) - summed
                grad_uy = ct - shifted_east(ct, rb)
                gu = coef(b0, 0) * (df1 - df) + coef(b0, 1) * grad_uy
                gv = coef(b0, 2) * grad_v + coef(b0, 3) * (ct1 - ct)
                GR[i + 1, 16 * g : 16 * g + 16, j * C : (j + 1) * C] = jnp.concatenate(
                    [gu, gv], 0
                ).astype(BF16)
                uf, va, ct, df, ra = uf1, va1, ct1, df1, ra1
            after.append((uf, va, ct, df, ra))
        return tuple(after)

    lax.fori_loop(0, n8, stencil_chunk, tuple(first))
    weight_chunk(n8, n8 - 1)

    scale = 1.0 / (R * n_lat * C * n_lon)
    acc = ACC[...] * scale
    acc = jnp.concatenate([acc, jnp.zeros((C - CHP, ft), F32)], 0)
    WS[...] = acc.T

    def rows_copy(peer, d, slot):
        src = WS.at[pl.ds(pl.multiple_of(peer * blk, blk), blk)]
        return pltpu.make_async_remote_copy(
            src_ref=src, dst_ref=RB.at[slot], send_sem=rs_s.at[d], recv_sem=rs_r.at[slot],
            device_id=(peer, lat), device_id_type=MESH,
        )

    @pl.loop(1, n_lon)
    def _(d):
        rows_copy(lax.rem(lon + d, n_lon), d, lon).start()

    @pl.loop(0, n8)
    def _(i):
        pltpu.make_async_copy(GR.at[i + 1], gr_out.at[i], gsem.at[i]).start()

    RB[lon] = WS[pl.ds(pl.multiple_of(lon * blk, blk), blk), :]

    @pl.loop(1, n_lon)
    def _(d):
        slot = lax.rem(lon + n_lon - d, n_lon)
        rows_copy(slot, d, slot).wait_recv()

    total = RB[0]
    for k in range(1, n_lon):
        total = total + RB[k]
    LB[lat] = total

    def lat_copy(d):
        return pltpu.make_async_remote_copy(
            src_ref=LB.at[lat], dst_ref=LB.at[lat], send_sem=ls_s.at[d], recv_sem=ls_r.at[d],
            device_id=(lon, lax.rem(lat + d, n_lat)), device_id_type=MESH,
        )

    for d in range(1, n_lat):
        lat_copy(d).start()
    for d in range(1, n_lat):
        lat_copy(d).wait_recv()
    total = LB[0]
    for k in range(1, n_lat):
        total = total + LB[k]
    pieces = [total[:, 16 * g : 16 * g + 8] for g in range(2)] + [total[:, 32:35]]
    pieces += [total[:, 16 * g + 8 : 16 * g + 16] for g in range(2)] + [total[:, 40:43]]
    wg_out[...] = jnp.concatenate(pieces + [total[:, 48:86]], 1)

    for d in range(1, n_lat):
        lat_copy(d).wait_send()

    @pl.loop(1, n_lon)
    def _(d):
        rows_copy(lax.rem(lon + d, n_lon), d, lon).wait_send()

    @pl.when(jnp.logical_not(top))
    def _():
        to_north.wait_send()
        to_nw.wait_send()

    @pl.when(top)
    def _():
        @pl.loop(1, n_lon)
        def _(d):
            fold_copy(lax.rem(lon + d, n_lon), d, lon).wait_send()

    @pl.when(jnp.logical_not(bottom))
    def _():
        to_south.wait_send()
        to_se.wait_send()

    to_east.wait_send()
    to_west.wait_send()
    wp_copy.wait()

    @pl.loop(0, n8)
    def _(i):
        pltpu.make_async_copy(GR.at[i + 1], gr_out.at[i], gsem.at[i]).wait()


def feature_kernel(gr, wp, out, held, sems):
    pieces, ft = sems.shape[0], held.shape[1]
    per = held.shape[0] // pieces
    in_slot = gr.shape[2] // per
    copies = []
    for i in range(pieces):
        at = slice(i * per, (i + 1) * per)
        cells = slice(i % in_slot * per, (i % in_slot + 1) * per)
        held[at, :] = lax.dot_general(
            gr[i // in_slot, :, cells], wp[...], (((0,), (0,)), ((), ())),
            preferred_element_type=F32,
        ).astype(BF16)
        copies.append(pltpu.make_async_copy(held.at[at], out.at[at], sems.at[i]))
        copies[-1].start()
    for copy in copies:
        copy.wait()


def per_device(n_lon, n_lat, features, head_weight, target, metrics, masks, partner):
    R, C, ft = features.shape
    ch = target.shape[0]
    blk = ft // n_lon
    n8 = R // 8
    cells = R * C
    hbm = pl.BlockSpec(memory_space=pl.ANY)
    vmem = pl.BlockSpec(memory_space=pltpu.VMEM)
    V = pltpu.VMEM
    D = pltpu.SemaphoreType.DMA
    gr, wp, wg = pl.pallas_call(
        grads_kernel,
        out_shape=(
            jax.ShapeDtypeStruct((n8, CHP, 8 * C), BF16),
            jax.ShapeDtypeStruct((CHP, ft), BF16),
            jax.ShapeDtypeStruct((blk, ch), F32),
        ),
        in_specs=[pl.BlockSpec(memory_space=pltpu.HBM)] * 6,
        out_specs=(hbm, hbm, vmem),
        scratch_shapes=[
            V((R, C, ft), BF16),
            V((ch, R, C), BF16),
            V(((ch + 4) * R, C), F32),
            V((6, R, C), F32),
            V((4, R, C), jnp.int32),
            V((ch, ft), BF16),
            V((n_lon, C), jnp.int32),
            V((CHP, ft), BF16),
            V(((R + 2) * ROW, C), F32),
            V((ROW, C), F32),
            V((2 * R, ft), BF16),
            V((ROW, C), F32),
            V((ROW, C), F32),
            V((32, C), F32),
            V((32, C), F32),
            V((24, C), F32),
            V((24, C), F32),
            V((n_lon, 24, C), F32),
            V((n8 + 1, CHP, 8 * C), BF16),
            V((CHP, ft), F32),
            V((ft, C), F32),
            V((n_lon, blk, C), F32),
            V((n_lat, blk, C), F32),
            D((R // 16,)), D((2,)), D((6,)), D((n8,)), D((6,)), D((6,)),
            D((n_lon,)), D((n_lon,)), D((n_lon,)), D((n_lon,)), D((n_lat,)), D((n_lat,)),
        ],
        compiler_params=pltpu.CompilerParams(
            collective_id=0, has_side_effects=True, vmem_limit_bytes=48 * 1024 * 1024
        ),
        cost_estimate=pl.CostEstimate(
            flops=4 * cells * ft * CHP, bytes_accessed=12 * 1024 * 1024, transcendentals=0
        ),
        name="grads_and_weight_grad",
    )(
        *(
            pltpu.with_memory_space_constraint(x, pltpu.HBM)
            for x in (
                features, target, metrics, masks, head_weight.T,
                partner.reshape(n_lon, C),
            )
        )
    )
    feature_grad = pl.pallas_call(
        feature_kernel,
        out_shape=jax.ShapeDtypeStruct((cells, ft), BF16),
        in_specs=[vmem, vmem],
        out_specs=hbm,
        scratch_shapes=[V((cells, ft), BF16), D((2 * n8,))],
        compiler_params=pltpu.CompilerParams(vmem_limit_bytes=32 * 1024 * 1024),
        cost_estimate=pl.CostEstimate(
            flops=2 * cells * ft * CHP, bytes_accessed=10 * 1024 * 1024, transcendentals=0
        ),
        name="feature_grad",
    )(gr, wp)
    return feature_grad.reshape(R, C, ft), wg


def solution(mesh):
    return jax.shard_map(
        functools.partial(per_device, mesh.shape["lon"], mesh.shape["lat"]),
        mesh=mesh,
        in_specs=(
            P("lat", "lon", None),
            P(),
            P(None, "lat", "lon"),
            P(None, "lat", "lon"),
            P(None, "lat", "lon"),
            P(),
        ),
        out_specs=(P("lat", "lon", None), P("lon", None)),
        check_vma=False,
    )
```

```python
import functools

import jax
import jax.numpy as jnp
from jax import lax
from jax.experimental import pallas as pl
from jax.experimental.pallas import tpu as pltpu
from jax.sharding import PartitionSpec as P

LEV = 19
CHP = 96
ROW = 56
MESH = pl.DeviceIdType.MESH
F32 = jnp.float32
BF16 = jnp.bfloat16
NT = (((1,), (1,)), ((), ()))
NN = (((1,), (0,)), ((), ()))


def lanes(shape):
    return lax.broadcasted_iota(jnp.int32, shape, len(shape) - 1)


def grads_kernel(
    feat, tgt, met, msk, wt, part, gr_out, wp_out, wg_out,
    F, Tb, Tf, M, K, Wv, Pv, Wp, EG, ED, FE, DX, HW, HE, CNW, CSE, FS, FB, GR, ACC, WS, RB, LB,
    fsem, lsem, gsem, hs, hr, fs_s, fs_r, rs_s, rs_r, ls_s, ls_r,
):
    n_lon, n_lat = lax.axis_size("lon"), lax.axis_size("lat")
    lon, lat = lax.axis_index("lon"), lax.axis_index("lat")
    R, C, ft = feat.shape
    n16 = R // 16
    n8 = R // 8
    blk = ft // n_lon
    top = lat == n_lat - 1
    bottom = lat == 0
    east = lax.rem(lon + 1, n_lon)
    west = lax.rem(lon + n_lon - 1, n_lon)
    up = lax.rem(lat + 1, n_lat)
    down = lax.rem(lat + n_lat - 1, n_lat)

    barrier = pltpu.get_barrier_semaphore()
    pl.semaphore_signal(barrier, inc=1, device_id=(east, lat), device_id_type=MESH)
    pl.semaphore_signal(barrier, inc=1, device_id=(west, lat), device_id_type=MESH)
    for d in range(1, n_lat):
        pl.semaphore_signal(
            barrier, inc=1, device_id=(lon, lax.rem(lat + d, n_lat)), device_id_type=MESH
        )
    pl.semaphore_signal(barrier, inc=1, device_id=(east, down), device_id_type=MESH)
    pl.semaphore_signal(barrier, inc=1, device_id=(west, up), device_id_type=MESH)

    def fcopy(c):
        at = pl.ds(c * 16, 16)
        return pltpu.make_async_copy(feat.at[at], F.at[at], fsem.at[c])

    small = [
        pltpu.make_async_copy(met, M, lsem.at[0]),
        pltpu.make_async_copy(msk, K, lsem.at[1]),
        pltpu.make_async_copy(wt, Wv, lsem.at[2]),
        pltpu.make_async_copy(part, Pv, lsem.at[3]),
        pltpu.make_async_copy(tgt, Tb.at[0 : 4 * LEV], lsem.at[4]),
    ]
    for copy in small:
        copy.start()
    for i in range(n16):
        fcopy((i + n16 - 1) % n16).start()

    @pl.when(bottom)
    def _():
        EG[0:ROW, :] = jnp.zeros((ROW, C), F32)
        CSE[...] = jnp.zeros_like(CSE)

    @pl.when(top)
    def _():
        EG[(R + 1) * ROW : (R + 2) * ROW, :] = jnp.zeros((ROW, C), F32)
        CNW[...] = jnp.zeros_like(CNW)

    @pl.loop(2, n_lon - 1)
    def _(d):
        pl.semaphore_signal(
            barrier, inc=1, device_id=(lax.rem(lon + d, n_lon), lat), device_id_type=MESH
        )

    small[0].wait()
    small[1].wait()
    for g in range(n8):
        at = slice(8 * g, 8 * g + 8)
        um, vm = K[0, at, :].astype(F32), K[1, at, :].astype(F32)
        qm, hm = K[2, at, :].astype(F32), K[3, at, :].astype(F32)
        area_h = M[5, at, :]
        qw = 2.0 * qm / M[4, at, :]
        coefs = (
            M[0, at, :] * um, M[1, at, :] * um, M[3, at, :] * vm, M[2, at, :] * vm,
            qw, hm / area_h, area_h * hm, qw,
        )
        for k, value in enumerate(coefs):
            EG[pl.ds((8 * g + 1) * ROW + 24 + k, 8, stride=ROW), :] = value

    small[2].wait()
    p = lax.broadcasted_iota(jnp.int32, (CHP, 4 * LEV), 0)
    c = lax.broadcasted_iota(jnp.int32, (CHP, 4 * LEV), 1)
    level = (p // 16) * 8 + p % 8
    pick = (p < 48) & (level < LEV) & (c == level + LEV * ((p // 8) % 2))
    pick = pick | ((p >= 48) & (c == p - 10))
    wp = lax.dot_general(
        jnp.where(pick, 1.0, 0.0).astype(BF16), Wv[...], NN, preferred_element_type=F32
    )
    Wp[...] = wp.astype(BF16)
    wp_copy = pltpu.make_async_copy(Wp, wp_out, lsem.at[5])
    wp_copy.start()
    small[3].wait()

    firsts = [0, LEV, 8, LEV + 8, 16, LEV + 16] + [2 * LEV + 8 * k for k in range(5)]
    Tb[4 * LEV :, :, :] = jnp.zeros((4, R, C), BF16)
    small[4].wait()

    def widen(i, _):
        at = pl.ds(pl.multiple_of(16 * i, 16), 16)
        for k, ch in enumerate(firsts):
            turned = jnp.swapaxes(Tb[ch : ch + 8, at, :].astype(F32), 0, 1)
            Tf[at, 8 * k : 8 * k + 8, :] = turned
        return 0

    lax.fori_loop(0, n16, widen, 0)

    q = lax.broadcasted_iota(jnp.int32, (16, 256), 0)
    cell = lax.broadcasted_iota(jnp.int32, (16, 256), 1)
    wanted = (q >> 1) * 16 + jnp.where((q & 1) == 1, 0, 128 + 15)
    choose = jnp.where(cell == wanted, 1.0, 0.0).astype(BF16)
    ED[...] = jnp.zeros_like(ED)

    def send(src, dst, k, device):
        return pltpu.make_async_remote_copy(
            src_ref=src, dst_ref=dst, send_sem=hs.at[k], recv_sem=hr.at[k],
            device_id=device, device_id_type=MESH,
        )

    south_row = EG.at[0:ROW]
    first_row = EG.at[ROW : 2 * ROW]
    last_row = EG.at[R * ROW : (R + 1) * ROW]
    north_row = EG.at[(R + 1) * ROW : (R + 2) * ROW]
    to_north = send(last_row, south_row, 0, (lon, up))
    to_south = send(first_row, north_row, 1, (lon, down))
    to_east = send(ED, HW, 2, (east, lat))
    to_west = send(ED, HE, 3, (west, lat))
    to_nw = send(EG.at[R * ROW + 24 : (R + 1) * ROW], CSE, 4, (west, up))
    to_se = send(EG.at[ROW : ROW + 32], CNW, 5, (east, down))

    def fold_copy(peer, d, slot):
        return pltpu.make_async_remote_copy(
            src_ref=FS, dst_ref=FB.at[slot], send_sem=fs_s.at[d], recv_sem=fs_r.at[slot],
            device_id=(peer, lat), device_id_type=MESH,
        )

    half = lanes((ROW, C)) >> 1

    def errors_chunk(i, _):
        chunk = (i + n16 - 1) % n16
        r0 = chunk * 16
        fcopy(chunk).wait()
        packed = ED[...]
        for j4 in range(4):
            cells = F[pl.ds(r0 + 4 * j4, 4), :, :].reshape(4 * C, ft)
            predicted = lax.dot_general(Wp[...], cells, NT, preferred_element_type=F32)
            for j in range(4):
                q = 4 * j4 + j
                r = r0 + q
                base = (r + 1) * ROW
                mine = predicted[0:88, j * C : (j + 1) * C] - Tf[r]
                for k in range(3):
                    EG[pl.ds(base + 8 * k, 8), :] = mine[16 * k : 16 * k + 8]
                    EG[pl.ds(base + 32 + 8 * k, 8), :] = mine[16 * k + 8 : 16 * k + 16]
                other = mine[48:88] * EG[pl.ds(base + 30, 1), :]
                other = jnp.concatenate([other, jnp.zeros((8, C), F32)], 0)
                GR[2 * chunk + q // 8 + 1, 48:CHP, (q % 8) * C : (q % 8 + 1) * C] = other.astype(BF16)
                packed = jnp.where(
                    half == r, pltpu.roll(EG[pl.ds(base, ROW), :], 2 * r + 1, 1), packed
                )
        ED[...] = packed

        if i == 1:
            pl.semaphore_wait(barrier, n_lon + n_lat)

            @pl.when(jnp.logical_not(top))
            def _():
                to_north.start()
                to_nw.start()

            @pl.when(top)
            def _():
                row = R * ROW
                flux = EG[row : row + 24, :] * EG[row + 24 : row + 25, :]
                sub = lax.broadcasted_iota(jnp.int32, (24, C), 0)
                FS[...] = jnp.where(sub == 23, EG[row + 28 : row + 29, :], flux)

                @pl.loop(1, n_lon)
                def _(d):
                    fold_copy(lax.rem(lon + d, n_lon), d, lon).start()

                FB[lon] = FS[...]

            @pl.when(jnp.logical_not(bottom))
            def _():
                to_south.start()
                to_se.start()

        return 0

    for i in range(n16):
        errors_chunk(i, 0)
    to_east.start()
    to_west.start()

    @pl.when(jnp.logical_not(bottom))
    def _():
        to_north.wait_recv()
        to_nw.wait_recv()

    def roll(x, by):
        return pltpu.roll(x, by, 1)

    def u_at(base, g):
        return EG[pl.ds(base + 8 * g, 8), :]

    def v_at(base, g):
        return EG[pl.ds(base + 32 + 8 * g, 8), :]

    def coef(base, k):
        return EG[pl.ds(base + 24 + k, 1), :]

    def west_of(x):
        return roll(x, 1)

    def east_of(x):
        return roll(x, C - 1)

    first = []
    for g in range(3):
        uf0 = u_at(ROW, g) * coef(ROW, 0)
        va0 = v_at(ROW, g) * coef(ROW, 3)
        ua0 = u_at(ROW, g) * coef(ROW, 1)
        before = v_at(0, g) * coef(0, 3)
        ct0 = coef(ROW, 5) * (ua0 - west_of(ua0) - va0 + before)
        df0 = coef(0, 7) * (u_at(0, g) * coef(0, 0) - uf0)
        first.append((uf0, va0, ct0, df0))

    ACC[...] = jnp.zeros_like(ACC)

    GR[0] = jnp.zeros(GR.shape[1:], BF16)

    def weight_chunk(slot, chunk):
        cells = F[8 * chunk : 8 * chunk + 8, :, :].reshape(8 * C, ft)
        ACC[...] += jnp.dot(GR[slot], cells, preferred_element_type=F32)
        rows = slice(8 * chunk, 8 * chunk + 8)
        sides = [F[rows, 0:16, :].reshape(128, ft), F[rows, C - 16 : C, :].reshape(128, ft)]
        FE[16 * chunk : 16 * chunk + 16, :] = jnp.dot(
            choose, jnp.concatenate(sides, 0), preferred_element_type=F32
        ).astype(BF16)

    def stencil_chunk(i, carry):
        last = i == n8 - 1

        if last:
            @pl.when(jnp.logical_not(top))
            def _():
                to_south.wait_recv()
                to_se.wait_recv()

            @pl.when(top)
            def _():
                @pl.loop(1, n_lon)
                def _(d):
                    slot = lax.rem(lon + n_lon - d, n_lon)
                    fold_copy(slot, d, slot).wait_recv()

                wide = (24, C)
                mirror = Pv[pl.ds(lon, 1), :]
                which = jnp.broadcast_to(mirror >> 7, wide)
                within = jnp.broadcast_to(mirror & 127, wide)

                found = jnp.zeros(wide, F32)
                for b in range(n_lon):
                    there = jnp.take_along_axis(FB[b], within, axis=1, mode="promise_in_bounds")
                    found = jnp.where(which == b, there, found)
                beyond = (R + 1) * ROW
                EG[beyond : beyond + 24, :] = -found
                EG[beyond + 24 : beyond + 25, :] = jnp.ones((1, C), F32)
                at = R * ROW + 31
                EG[at : at + 1, :] = EG[at : at + 1, :] + found[23:24]

        weight_chunk(i, max(i - 1, 0))
        after = []
        for g in range(3):
            uf, va, ct, df = carry[g]
            for j in range(8):
                r = 8 * i + j
                b0 = (r + 1) * ROW
                b1 = (r + 2) * ROW
                u1, v1 = u_at(b1, g), v_at(b1, g)
                uf1, ua1, va1 = u1 * coef(b1, 0), u1 * coef(b1, 1), v1 * coef(b1, 3)
                df1 = coef(b0, 7) * (uf - uf1)
                ct1 = coef(b1, 5) * (ua1 - west_of(ua1) - va1 + va)
                vf = v_at(b0, g) * coef(b0, 2)
                summed = coef(b0, 4) * (east_of(vf) - vf)
                grad_v = west_of(summed) - summed
                grad_uy = ct - east_of(ct)
                gu = coef(b0, 0) * (df1 - df) + coef(b0, 1) * grad_uy
                gv = coef(b0, 2) * grad_v + coef(b0, 3) * (ct1 - ct)
                GR[i + 1, 16 * g : 16 * g + 16, j * C : (j + 1) * C] = jnp.concatenate(
                    [gu, gv], 0
                ).astype(BF16)
                uf, va, ct, df = uf1, va1, ct1, df1
            after.append((uf, va, ct, df))
        return tuple(after)

    carry = tuple(first)
    for i in range(n8):
        carry = stencil_chunk(i, carry)
    weight_chunk(n8, n8 - 1)

    to_east.wait_recv()
    to_west.wait_recv()
    lane = lanes((24, C))
    even = (lane & 1) == 0
    ends = lane >= 2 * R - 2
    ed = ED[...]
    swap = jnp.where((lanes((ROW, C)) & 1) == 0, roll(ed, C - 1), roll(ed, 1))
    beside = jnp.where((lanes((ROW, C)) & 1) == 0, roll(HE[...], C - 1), roll(HW[...], 1))

    def part(x, k):
        return x[24 + k : 25 + k]

    u_own, v_own = ed[0:24], ed[32:56]
    u_swap, v_swap = swap[0:24], swap[32:56]
    u_side, v_side = beside[0:24], beside[32:56]
    ua_own, ua_swap, ua_side = u_own * part(ed, 1), u_swap * part(swap, 1), u_side * part(beside, 1)
    vf_own, vf_swap, vf_side = v_own * part(ed, 2), v_swap * part(swap, 2), v_side * part(beside, 2)
    va_swap, va_side = v_swap * part(swap, 3), v_side * part(beside, 3)
    corner = CSE[8:32, :] * CSE[3:4, :]
    below = EG[32:56, :] * EG[27:28, :]
    va_side0 = jnp.where(lane == 0, corner, roll(va_side, 2))
    va_swap0 = jnp.where(lane == 0, below, roll(va_swap, 2))
    ct_side = part(beside, 5) * (ua_side - ua_own - va_side + va_side0)
    ct_swap = part(swap, 5) * (ua_swap - ua_own - va_swap + va_swap0)
    gap = part(ed, 5) * (ua_swap - ua_side)
    beyond = (R + 1) * ROW
    ua_up = EG[beyond : beyond + 24, :] * EG[beyond + 25 : beyond + 26, :]
    ua_far = CNW[0:24, :] * CNW[25:26, :]
    hw_up = jnp.broadcast_to(EG[beyond + 29 : beyond + 30, :], (24, C))
    gap_up = hw_up * roll(ua_up - ua_far, 1)
    gap_up = jnp.where(ends, roll(gap_up, 2 * R - 1), roll(gap, C - 2))
    fix_u = part(ed, 1) * jnp.where(even, ct_swap - ct_side, gap)
    flux_e = part(ed, 4) * (vf_swap - vf_side)
    flux_w = part(beside, 4) * (vf_own - vf_side) - part(swap, 4) * (vf_own - vf_swap)
    fix_v = part(ed, 2) * jnp.where(even, flux_e, flux_w)
    fix_v = fix_v + jnp.where(even, 0.0, part(ed, 3) * (gap_up - gap))
    fix = []
    for g in range(3):
        fix += [fix_u[8 * g : 8 * g + 8], fix_v[8 * g : 8 * g + 8]]
    fix = jnp.concatenate(fix, 0)
    DX[...] = fix
    ACC[0:48, :] += jnp.dot(fix[:, 0 : 2 * R].astype(BF16), FE[...], preferred_element_type=F32)

    scale = 1.0 / (R * n_lat * C * n_lon)
    acc = ACC[...] * scale
    acc = jnp.concatenate([acc, jnp.zeros((C - CHP, ft), F32)], 0)
    WS[...] = acc.T

    def rows_copy(peer, d, slot):
        src = WS.at[pl.ds(pl.multiple_of(peer * blk, blk), blk)]
        return pltpu.make_async_remote_copy(
            src_ref=src, dst_ref=RB.at[slot], send_sem=rs_s.at[d], recv_sem=rs_r.at[slot],
            device_id=(peer, lat), device_id_type=MESH,
        )

    @pl.loop(1, n_lon)
    def _(d):
        rows_copy(lax.rem(lon + d, n_lon), d, lon).start()

    @pl.loop(0, n8)
    def _(i):
        at_ends = lanes((48, C))
        at_ends = (at_ends == 0) | (at_ends == C - 1)
        for j in range(8):
            here = (i + 1, slice(0, 48), slice(j * C, (j + 1) * C))
            held = GR[here].astype(F32)
            more = roll(DX[...], C - 1 - 2 * (8 * i + j))
            GR[here] = jnp.where(at_ends, held + more, held).astype(BF16)
        pltpu.make_async_copy(GR.at[i + 1], gr_out.at[i], gsem.at[i]).start()

    RB[lon] = WS[pl.ds(pl.multiple_of(lon * blk, blk), blk), :]

    @pl.loop(1, n_lon)
    def _(d):
        slot = lax.rem(lon + n_lon - d, n_lon)
        rows_copy(slot, d, slot).wait_recv()

    total = RB[0]
    for k in range(1, n_lon):
        total = total + RB[k]
    LB[lat] = total

    def lat_copy(d):
        return pltpu.make_async_remote_copy(
            src_ref=LB.at[lat], dst_ref=LB.at[lat], send_sem=ls_s.at[d], recv_sem=ls_r.at[d],
            device_id=(lon, lax.rem(lat + d, n_lat)), device_id_type=MESH,
        )

    def when_upper(d):
        return pl.when(lax.rem(lat + d, n_lat) >= n_lat // 2)

    for d in range(1, n_lat):

        @when_upper(d)
        def _(d=d):
            lat_copy(d).start()

    wg_out[...] = jnp.zeros_like(wg_out)

    @when_upper(0)
    def _():
        for d in range(1, n_lat):
            lat_copy(d).wait_recv()
        total = LB[0]
        for k in range(1, n_lat):
            total = total + LB[k]
        pieces = [total[:, 16 * g : 16 * g + 8] for g in range(2)] + [total[:, 32:35]]
        pieces += [total[:, 16 * g + 8 : 16 * g + 16] for g in range(2)] + [total[:, 40:43]]
        wg_out[...] = jnp.concatenate(pieces + [total[:, 48:86]], 1)

    for d in range(1, n_lat):

        @when_upper(d)
        def _(d=d):
            lat_copy(d).wait_send()

    @pl.loop(1, n_lon)
    def _(d):
        rows_copy(lax.rem(lon + d, n_lon), d, lon).wait_send()

    @pl.when(jnp.logical_not(top))
    def _():
        to_north.wait_send()
        to_nw.wait_send()

    @pl.when(top)
    def _():
        @pl.loop(1, n_lon)
        def _(d):
            fold_copy(lax.rem(lon + d, n_lon), d, lon).wait_send()

    @pl.when(jnp.logical_not(bottom))
    def _():
        to_south.wait_send()
        to_se.wait_send()

    to_east.wait_send()
    to_west.wait_send()
    wp_copy.wait()

    @pl.loop(0, n8)
    def _(i):
        pltpu.make_async_copy(GR.at[i + 1], gr_out.at[i], gsem.at[i]).wait()


def feature_kernel(gr, wp, out, held, sems):
    pieces, ft = sems.shape[0], held.shape[1]
    per = held.shape[0] // pieces
    in_slot = gr.shape[2] // per
    copies = []
    for i in range(pieces):
        at = slice(i * per, (i + 1) * per)
        cells = slice(i % in_slot * per, (i % in_slot + 1) * per)
        held[at, :] = lax.dot_general(
            gr[i // in_slot, :, cells], wp[...], (((0,), (0,)), ((), ())),
            preferred_element_type=F32,
        ).astype(BF16)
        copies.append(pltpu.make_async_copy(held.at[at], out.at[at], sems.at[i]))
        copies[-1].start()
    for copy in copies:
        copy.wait()


def per_device(n_lon, n_lat, features, head_weight, target, metrics, masks, partner):
    R, C, ft = features.shape
    ch = target.shape[0]
    blk = ft // n_lon
    n8 = R // 8
    cells = R * C
    hbm = pl.BlockSpec(memory_space=pl.ANY)
    vmem = pl.BlockSpec(memory_space=pltpu.VMEM)
    V = pltpu.VMEM
    D = pltpu.SemaphoreType.DMA
    gr, wp, wg = pl.pallas_call(
        grads_kernel,
        out_shape=(
            jax.ShapeDtypeStruct((n8, CHP, 8 * C), BF16),
            jax.ShapeDtypeStruct((CHP, ft), BF16),
            jax.ShapeDtypeStruct((blk, ch), F32),
        ),
        in_specs=[pl.BlockSpec(memory_space=pltpu.HBM)] * 6,
        out_specs=(hbm, hbm, vmem),
        scratch_shapes=[
            V((R, C, ft), BF16),
            V((ch + 4, R, C), BF16),
            V((R, 88, C), F32),
            V((6, R, C), F32),
            V((4, R, C), jnp.int32),
            V((ch, ft), BF16),
            V((n_lon, C), jnp.int32),
            V((CHP, ft), BF16),
            V(((R + 2) * ROW, C), F32),
            V((ROW, C), F32),
            V((2 * R, ft), BF16),
            V((48, C), F32),
            V((ROW, C), F32),
            V((ROW, C), F32),
            V((32, C), F32),
            V((32, C), F32),
            V((24, C), F32),
            V((n_lon, 24, C), F32),
            V((n8 + 1, CHP, 8 * C), BF16),
            V((CHP, ft), F32),
            V((ft, C), F32),
            V((n_lon, blk, C), F32),
            V((n_lat, blk, C), F32),
            D((R // 16,)), D((6,)), D((n8,)), D((6,)), D((6,)),
            D((n_lon,)), D((n_lon,)), D((n_lon,)), D((n_lon,)), D((n_lat,)), D((n_lat,)),
        ],
        compiler_params=pltpu.CompilerParams(
            collective_id=0, has_side_effects=True, vmem_limit_bytes=48 * 1024 * 1024
        ),
        cost_estimate=pl.CostEstimate(
            flops=4 * cells * ft * CHP, bytes_accessed=12 * 1024 * 1024, transcendentals=0
        ),
        name="grads_and_weight_grad",
    )(
        *(
            pltpu.with_memory_space_constraint(x, pltpu.HBM)
            for x in (
                features, target, metrics, masks, head_weight.T,
                partner.reshape(n_lon, C),
            )
        )
    )
    feature_grad = pl.pallas_call(
        feature_kernel,
        out_shape=jax.ShapeDtypeStruct((cells, ft), BF16),
        in_specs=[vmem, vmem],
        out_specs=hbm,
        scratch_shapes=[V((cells, ft), BF16), D((2 * n8,))],
        compiler_params=pltpu.CompilerParams(vmem_limit_bytes=32 * 1024 * 1024),
        cost_estimate=pl.CostEstimate(
            flops=2 * cells * ft * CHP, bytes_accessed=10 * 1024 * 1024, transcendentals=0
        ),
        name="feature_grad",
    )(gr, wp)
    down = [(k, k - n_lat // 2) for k in range(n_lat // 2, n_lat)]
    weight_grad = wg + lax.ppermute(wg, "lat", down)
    return feature_grad.reshape(R, C, ft), weight_grad


def solution(mesh):
    return jax.shard_map(
        functools.partial(per_device, mesh.shape["lon"], mesh.shape["lat"]),
        mesh=mesh,
        in_specs=(
            P("lat", "lon", None),
            P(),
            P(None, "lat", "lon"),
            P(None, "lat", "lon"),
            P(None, "lat", "lon"),
            P(),
        ),
        out_specs=(P("lat", "lon", None), P("lon", None)),
        check_vma=False,
    )
```

```python
import functools

import jax
import jax.numpy as jnp
from jax import lax
from jax.experimental import pallas as pl
from jax.experimental.pallas import tpu as pltpu
from jax.sharding import PartitionSpec as P

LEV = 19
CHP = 96
ROW = 56
MESH = pl.DeviceIdType.MESH
F32 = jnp.float32
BF16 = jnp.bfloat16
NT = (((1,), (1,)), ((), ()))
NN = (((1,), (0,)), ((), ()))


def lanes(shape):
    return lax.broadcasted_iota(jnp.int32, shape, len(shape) - 1)


def grads_kernel(
    feat, tgt, met, msk, wt, part, gr_out, wp_out, wg_out,
    F, FR, RS, Tb, Tf, M, K, Wv, Pv, Wp, EG, ED, FE, FT, DX, HW, HE, CNW, CSE, FS, FB, GR, ACC, WS, RB, LB,
    fsem, esem, lsem, gsem, hs, hr, fs_s, fs_r, rs_s, rs_r, ls_s, ls_r,
):
    n_lon, n_lat = lax.axis_size("lon"), lax.axis_size("lat")
    lon, lat = lax.axis_index("lon"), lax.axis_index("lat")
    R, C, ft = feat.shape
    n16 = R // 16
    n8 = R // 8
    blk = ft // n_lon
    top = lat == n_lat - 1
    bottom = lat == 0
    east = lax.rem(lon + 1, n_lon)
    west = lax.rem(lon + n_lon - 1, n_lon)
    up = lax.rem(lat + 1, n_lat)
    down = lax.rem(lat + n_lat - 1, n_lat)

    barrier = pltpu.get_barrier_semaphore()
    pl.semaphore_signal(barrier, inc=1, device_id=(east, lat), device_id_type=MESH)
    pl.semaphore_signal(barrier, inc=1, device_id=(west, lat), device_id_type=MESH)
    for d in range(1, n_lat):
        pl.semaphore_signal(
            barrier, inc=1, device_id=(lon, lax.rem(lat + d, n_lat)), device_id_type=MESH
        )
    pl.semaphore_signal(barrier, inc=1, device_id=(east, down), device_id_type=MESH)
    pl.semaphore_signal(barrier, inc=1, device_id=(west, up), device_id_type=MESH)

    def fcopy(c):
        at = (pl.ds(c * 16, 16), pl.ds(16, C - 32))
        return pltpu.make_async_copy(feat.at[at], F.at[at], fsem.at[c])

    def ecopy(k):
        at = (pl.ds(0, R), pl.ds(k * (C - 16), 16))
        return pltpu.make_async_copy(feat.at[at], F.at[at], esem.at[k])

    rows_in = [
        pltpu.make_async_copy(feat.at[0:1], FR.at[0:1], esem.at[2]),
        pltpu.make_async_copy(feat.at[R - 1 : R], FR.at[1:2], esem.at[3]),
    ]
    small = [
        pltpu.make_async_copy(met, M, lsem.at[0]),
        pltpu.make_async_copy(msk, K, lsem.at[1]),
        pltpu.make_async_copy(wt, Wv, lsem.at[2]),
        pltpu.make_async_copy(part, Pv, lsem.at[3]),
        pltpu.make_async_copy(tgt, Tb.at[0 : 4 * LEV], lsem.at[4]),
    ]
    for copy in small:
        copy.start()
    for copy in rows_in:
        copy.start()
    ecopy(0).start()
    ecopy(1).start()
    for i in range(n16):
        fcopy((i + n16 - 1) % n16).start()

    @pl.when(bottom)
    def _():
        EG[0:ROW, :] = jnp.zeros((ROW, C), F32)
        CSE[...] = jnp.zeros_like(CSE)

    @pl.when(top)
    def _():
        EG[(R + 1) * ROW : (R + 2) * ROW, :] = jnp.zeros((ROW, C), F32)
        CNW[...] = jnp.zeros_like(CNW)

    @pl.loop(2, n_lon - 1)
    def _(d):
        pl.semaphore_signal(
            barrier, inc=1, device_id=(lax.rem(lon + d, n_lon), lat), device_id_type=MESH
        )

    small[0].wait()
    small[1].wait()
    for g in range(n8):
        at = slice(8 * g, 8 * g + 8)
        um, vm = K[0, at, :].astype(F32), K[1, at, :].astype(F32)
        qm, hm = K[2, at, :].astype(F32), K[3, at, :].astype(F32)
        area_h = M[5, at, :]
        qw = 2.0 * qm / M[4, at, :]
        coefs = (
            M[0, at, :] * um, M[1, at, :] * um, M[3, at, :] * vm, M[2, at, :] * vm,
            qw, hm / area_h, area_h * hm, qw,
        )
        for k, value in enumerate(coefs):
            EG[pl.ds((8 * g + 1) * ROW + 24 + k, 8, stride=ROW), :] = value

    small[2].wait()
    p = lax.broadcasted_iota(jnp.int32, (CHP, 4 * LEV), 0)
    c = lax.broadcasted_iota(jnp.int32, (CHP, 4 * LEV), 1)
    level = (p // 16) * 8 + p % 8
    pick = (p < 48) & (level < LEV) & (c == level + LEV * ((p // 8) % 2))
    pick = pick | ((p >= 48) & (c == p - 10))
    wp = lax.dot_general(
        jnp.where(pick, 1.0, 0.0).astype(BF16), Wv[...], NN, preferred_element_type=F32
    )
    Wp[...] = wp.astype(BF16)
    wp_copy = pltpu.make_async_copy(Wp, wp_out, lsem.at[5])
    wp_copy.start()
    small[3].wait()

    firsts = [0, LEV, 8, LEV + 8, 16, LEV + 16] + [2 * LEV + 8 * k for k in range(5)]
    Tb[4 * LEV :, :, :] = jnp.zeros((4, R, C), BF16)
    small[4].wait()

    def widen(i, _):
        at = pl.ds(pl.multiple_of(16 * i, 16), 16)
        for k, ch in enumerate(firsts):
            turned = jnp.swapaxes(Tb[ch : ch + 8, at, :].astype(F32), 0, 1)
            Tf[at, 8 * k : 8 * k + 8, :] = turned
        return 0

    lax.fori_loop(0, n16, widen, 0)

    half8 = lanes((8, C)) >> 1

    def pack(i, packed):
        packed = list(packed)
        for j in range(16):
            r = 16 * i + j
            base = pl.multiple_of((r + 1) * ROW, 8)
            rows = [Tf[r, 8 * k : 8 * k + 8, :] for k in range(6)]
            rows.append(EG[pl.ds(base + 24, 8), :])
            by = 2 * r + 1
            packed = [
                jnp.where(half8 == r, pltpu.roll(x, by, 1), y) for x, y in zip(rows, packed)
            ]
        return tuple(packed)

    packed = lax.fori_loop(0, n16, pack, (jnp.zeros((8, C), F32),) * 7)
    for copy in rows_in:
        copy.wait()
    at_rows = lax.dot_general(
        Wp[0:48, :], FR[...].reshape(2 * C, ft), NT, preferred_element_type=F32
    )
    for k, r in enumerate((0, R - 1)):
        found = at_rows[:, k * C : (k + 1) * C] - Tf[r, 0:48, :]
        to = k * ROW
        for g in range(3):
            RS[to + 8 * g : to + 8 * g + 8, :] = found[16 * g : 16 * g + 8]
            RS[to + 32 + 8 * g : to + 40 + 8 * g, :] = found[16 * g + 8 : 16 * g + 16]
        RS[to + 24 : to + 32, :] = EG[(r + 1) * ROW + 24 : (r + 1) * ROW + 32, :]

    q = lax.broadcasted_iota(jnp.int32, (32, 512), 0)
    cell = lax.broadcasted_iota(jnp.int32, (32, 512), 1)
    wanted = (q >> 1) * 16 + jnp.where((q & 1) == 1, 0, 256 + 15)
    choose = jnp.where(cell == wanted, 1.0, 0.0).astype(BF16)
    ecopy(0).wait()
    ecopy(1).wait()
    for i in range(n16):
        rows = slice(16 * i, 16 * i + 16)
        sides = [F[rows, 0:16, :].reshape(256, ft), F[rows, C - 16 : C, :].reshape(256, ft)]
        FE[32 * i : 32 * i + 32, :] = jnp.dot(
            choose, jnp.concatenate(sides, 0), preferred_element_type=F32
        ).astype(BF16)
    at_edges = lax.dot_general(Wp[0:48, :], FE[...], NT, preferred_element_type=F32)
    ED[...] = jnp.zeros_like(ED)
    for k in range(6):
        to = 8 * (k // 2) + 32 * (k % 2)
        ED[to : to + 8, 0 : 2 * R] = at_edges[8 * k : 8 * k + 8] - packed[k][:, 0 : 2 * R]
    ED[24:32, :] = packed[6]

    def send(src, dst, k, device):
        return pltpu.make_async_remote_copy(
            src_ref=src, dst_ref=dst, send_sem=hs.at[k], recv_sem=hr.at[k],
            device_id=device, device_id_type=MESH,
        )

    south_row = EG.at[0:ROW]
    first_row = RS.at[0:ROW]
    last_row = RS.at[ROW : 2 * ROW]
    north_row = EG.at[(R + 1) * ROW : (R + 2) * ROW]
    to_north = send(last_row, south_row, 0, (lon, up))
    to_south = send(first_row, north_row, 1, (lon, down))
    to_east = send(ED, HW, 2, (east, lat))
    to_west = send(ED, HE, 3, (west, lat))
    to_nw = send(RS.at[ROW + 24 : 2 * ROW], CSE, 4, (west, up))
    to_se = send(RS.at[0:32], CNW, 5, (east, down))

    def fold_copy(peer):
        return pltpu.make_async_remote_copy(
            src_ref=FS, dst_ref=FB.at[pl.ds(pl.multiple_of(lon * 24, 8), 24)],
            send_sem=fs_s, recv_sem=fs_r, device_id=(peer, lat), device_id_type=MESH,
        )

    others = pl.ds(0, (n_lon - 1) * 24)
    fold_all = pltpu.make_async_remote_copy(
        src_ref=FB.at[others], dst_ref=FB.at[others], send_sem=fs_s, recv_sem=fs_r,
        device_id=(east, lat), device_id_type=MESH,
    )

    pl.semaphore_wait(barrier, n_lon + n_lat)

    @pl.when(jnp.logical_not(top))
    def _():
        to_nw.start()
        to_north.start()

    @pl.when(jnp.logical_not(bottom))
    def _():
        to_se.start()
        to_south.start()

    to_east.start()
    to_west.start()

    @pl.when(top)
    def _():
        flux = RS[ROW : ROW + 24, :] * RS[ROW + 24 : ROW + 25, :]
        sub = lax.broadcasted_iota(jnp.int32, (24, C), 0)
        FS[...] = jnp.where(sub == 23, RS[ROW + 28 : ROW + 29, :], flux)

        @pl.loop(1, n_lon)
        def _(d):
            fold_copy(lax.rem(lon + d, n_lon)).start()

        FB[pl.ds(pl.multiple_of(lon * 24, 8), 24), :] = FS[...]

    def errors_chunk(i, _):
        chunk = (i + n16 - 1) % n16
        r0 = chunk * 16
        fcopy(chunk).wait()
        for j4 in range(4):
            cells = F[pl.ds(r0 + 4 * j4, 4), :, :].reshape(4 * C, ft)
            predicted = lax.dot_general(Wp[...], cells, NT, preferred_element_type=F32)
            for j in range(4):
                q = 4 * j4 + j
                r = r0 + q
                base = (r + 1) * ROW
                mine = predicted[0:88, j * C : (j + 1) * C] - Tf[r]
                for k in range(3):
                    EG[pl.ds(base + 8 * k, 8), :] = mine[16 * k : 16 * k + 8]
                    EG[pl.ds(base + 32 + 8 * k, 8), :] = mine[16 * k + 8 : 16 * k + 16]
                other = mine[48:88] * EG[pl.ds(base + 30, 1), :]
                other = jnp.concatenate([other, jnp.zeros((8, C), F32)], 0)
                GR[2 * chunk + q // 8 + 1, 48:CHP, (q % 8) * C : (q % 8 + 1) * C] = other.astype(BF16)

        return 0

    for i in range(n16):
        errors_chunk(i, 0)

    def roll(x, by):
        return pltpu.roll(x, by, 1)

    def u_at(base, g):
        return EG[pl.ds(base + 8 * g, 8), :]

    def v_at(base, g):
        return EG[pl.ds(base + 32 + 8 * g, 8), :]

    def coef(base, k):
        return EG[pl.ds(base + 24 + k, 1), :]

    def west_of(x):
        return roll(x, 1)

    def east_of(x):
        return roll(x, C - 1)

    def state_at(r):
        b0, b1 = r * ROW, (r + 1) * ROW
        state = []
        for g in range(3):
            uf = u_at(b1, g) * coef(b1, 0)
            va = v_at(b1, g) * coef(b1, 3)
            ua = u_at(b1, g) * coef(b1, 1)
            before = v_at(b0, g) * coef(b0, 3)
            ct = coef(b1, 5) * (ua - west_of(ua) - va + before)
            df = coef(b0, 7) * (u_at(b0, g) * coef(b0, 0) - uf)
            state.append((uf, va, ct, df))
        return state

    ACC[...] = jnp.zeros_like(ACC)


    def weight_chunk(slot, chunk):
        cells = F[8 * chunk : 8 * chunk + 8, :, :].reshape(8 * C, ft)
        ACC[...] += jnp.dot(GR[slot], cells, preferred_element_type=F32)

    def stencil_chunk(i, carry, done):
        last = i == n8 - 1

        if last:
            @pl.when(jnp.logical_not(top))
            def _():
                to_south.wait_recv()

            @pl.when(top)
            def _():
                fold_all.wait_recv()

                wide = (24, C)
                mirror = Pv[pl.ds(lon, 1), :]
                which = jnp.broadcast_to(mirror >> 7, wide)
                within = jnp.broadcast_to(mirror & 127, wide)

                found = jnp.zeros(wide, F32)
                for b in range(n_lon):
                    there = jnp.take_along_axis(
                        FB[24 * b : 24 * b + 24, :], within, axis=1, mode="promise_in_bounds"
                    )
                    found = jnp.where(which == b, there, found)
                beyond = (R + 1) * ROW
                EG[beyond : beyond + 24, :] = -found
                EG[beyond + 24 : beyond + 25, :] = jnp.ones((1, C), F32)
                at = R * ROW + 31
                EG[at : at + 1, :] = EG[at : at + 1, :] + found[23:24]

        if done is not None:
            weight_chunk(done + 1, done)
        after = []
        for g in range(3):
            uf, va, ct, df = carry[g]
            for j in range(8):
                r = 8 * i + j
                b0 = (r + 1) * ROW
                b1 = (r + 2) * ROW
                u1, v1 = u_at(b1, g), v_at(b1, g)
                uf1, ua1, va1 = u1 * coef(b1, 0), u1 * coef(b1, 1), v1 * coef(b1, 3)
                df1 = coef(b0, 7) * (uf - uf1)
                ct1 = coef(b1, 5) * (ua1 - west_of(ua1) - va1 + va)
                vf = v_at(b0, g) * coef(b0, 2)
                summed = coef(b0, 4) * (east_of(vf) - vf)
                grad_v = west_of(summed) - summed
                grad_uy = ct - east_of(ct)
                gu = coef(b0, 0) * (df1 - df) + coef(b0, 1) * grad_uy
                gv = coef(b0, 2) * grad_v + coef(b0, 3) * (ct1 - ct)
                GR[i + 1, 16 * g : 16 * g + 16, j * C : (j + 1) * C] = jnp.concatenate(
                    [gu, gv], 0
                ).astype(BF16)
                uf, va, ct, df = uf1, va1, ct1, df1
            after.append((uf, va, ct, df))
        return tuple(after)

    carry, done = state_at(8), None
    for i in [*range(1, n8 - 1), 0, n8 - 1]:
        if i == 0:
            kept = carry

            @pl.when(jnp.logical_not(bottom))
            def _():
                to_north.wait_recv()

            carry = state_at(0)
        elif i == n8 - 1:
            carry = kept
        carry = stencil_chunk(i, carry, done)
        done = i
    weight_chunk(done + 1, done)

    lane = lanes((24, C))
    even = (lane & 1) == 0
    even_row = (lanes((ROW, C)) & 1) == 0
    ends = lane >= 2 * R - 2
    ed = ED[...]
    swap = jnp.where(even_row, roll(ed, C - 1), roll(ed, 1))

    def part(x, k):
        return x[24 + k : 25 + k]

    u_own, v_own = ed[0:24], ed[32:56]
    u_swap, v_swap = swap[0:24], swap[32:56]
    ua_own, ua_swap = u_own * part(ed, 1), u_swap * part(swap, 1)
    vf_own, vf_swap = v_own * part(ed, 2), v_swap * part(swap, 2)
    va_swap = v_swap * part(swap, 3)
    below = EG[32:56, :] * EG[27:28, :]
    ct_swap = part(swap, 5) * (ua_swap - ua_own - va_swap + jnp.where(lane == 0, below, roll(va_swap, 2)))
    flux_swap = part(swap, 4) * (vf_own - vf_swap)
    beyond = (R + 1) * ROW
    ua_up = EG[beyond : beyond + 24, :] * EG[beyond + 25 : beyond + 26, :]
    hw_up = jnp.broadcast_to(EG[beyond + 29 : beyond + 30, :], (24, C))

    scale = 1.0 / (R * n_lat * C * n_lon)
    acc = jnp.concatenate([ACC[...] * scale, jnp.zeros((C - CHP, ft), F32)], 0)
    WS[...] = acc.T
    FT[...] = FE[...].T

    to_east.wait_recv()
    to_west.wait_recv()

    @pl.when(jnp.logical_not(bottom))
    def _():
        to_nw.wait_recv()

    @pl.when(jnp.logical_not(top))
    def _():
        to_se.wait_recv()

    corner = CSE[8:32, :] * CSE[3:4, :]
    ua_far = CNW[0:24, :] * CNW[25:26, :]
    gap_top = roll(hw_up * roll(ua_up - ua_far, 1), 2 * R - 1)
    beside = jnp.where(even_row, roll(HE[...], C - 1), roll(HW[...], 1))
    u_side, v_side = beside[0:24], beside[32:56]
    ua_side, vf_side = u_side * part(beside, 1), v_side * part(beside, 2)
    va_side = v_side * part(beside, 3)
    va_side0 = jnp.where(lane == 0, corner, roll(va_side, 2))
    ct_side = part(beside, 5) * (ua_side - ua_own - va_side + va_side0)
    flux_e = part(ed, 4) * (vf_swap - vf_side)
    gap = part(ed, 5) * (ua_swap - ua_side)
    gap_up = jnp.where(ends, gap_top, roll(gap, C - 2))
    flux_w = part(beside, 4) * (vf_own - vf_side) - flux_swap
    fix_u = part(ed, 1) * jnp.where(even, ct_swap - ct_side, gap)
    fix_v = part(ed, 2) * jnp.where(even, flux_e, flux_w)
    fix_v = fix_v + jnp.where(even, 0.0, part(ed, 3) * (gap_up - gap))
    fix = []
    for g in range(3):
        fix += [fix_u[8 * g : 8 * g + 8], fix_v[8 * g : 8 * g + 8]]
    fix = jnp.concatenate(fix, 0)
    DX[...] = fix
    more = lax.dot_general(
        FT[...], fix[:, 0 : 2 * R].astype(BF16), NT, preferred_element_type=F32
    )
    WS[:, 0:48] += more * scale

    def rows_copy(peer):
        src = WS.at[pl.ds(pl.multiple_of(peer * blk, blk), blk)]
        dst = RB.at[pl.ds(pl.multiple_of(lon * blk, blk), blk)]
        return pltpu.make_async_remote_copy(
            src_ref=src, dst_ref=dst, send_sem=rs_s, recv_sem=rs_r,
            device_id=(peer, lat), device_id_type=MESH,
        )

    rows_all = pltpu.make_async_remote_copy(
        src_ref=WS.at[0 : (n_lon - 1) * blk], dst_ref=RB.at[0 : (n_lon - 1) * blk],
        send_sem=rs_s, recv_sem=rs_r, device_id=(east, lat), device_id_type=MESH,
    )

    @pl.loop(1, n_lon)
    def _(d):
        rows_copy(lax.rem(lon + d, n_lon)).start()

    @pl.loop(0, n8)
    def _(i):
        at_ends = lanes((48, C))
        at_ends = (at_ends == 0) | (at_ends == C - 1)
        for j in range(8):
            here = (i + 1, slice(0, 48), slice(j * C, (j + 1) * C))
            held = GR[here].astype(F32)
            more = roll(DX[...], C - 1 - 2 * (8 * i + j))
            GR[here] = jnp.where(at_ends, held + more, held).astype(BF16)
        pltpu.make_async_copy(GR.at[i + 1], gr_out.at[i], gsem.at[i]).start()

    here = pl.ds(pl.multiple_of(lon * blk, blk), blk)
    RB[here, :] = WS[here, :]

    rows_all.wait_recv()
    total = RB[0:blk, :]
    for k in range(1, n_lon):
        total = total + RB[k * blk : (k + 1) * blk, :]
    LB[lat] = total

    def lat_copy(d):
        return pltpu.make_async_remote_copy(
            src_ref=LB.at[lat], dst_ref=LB.at[lat], send_sem=ls_s.at[d], recv_sem=ls_r.at[d],
            device_id=(lon, lax.rem(lat + d, n_lat)), device_id_type=MESH,
        )

    def when_upper(d):
        return pl.when(lax.rem(lat + d, n_lat) >= n_lat // 2)

    for d in range(1, n_lat):

        @when_upper(d)
        def _(d=d):
            lat_copy(d).start()

    wg_out[...] = jnp.zeros_like(wg_out)

    @when_upper(0)
    def _():
        for d in range(1, n_lat):
            lat_copy(d).wait_recv()
        total = LB[0]
        for k in range(1, n_lat):
            total = total + LB[k]
        pieces = [total[:, 16 * g : 16 * g + 8] for g in range(2)] + [total[:, 32:35]]
        pieces += [total[:, 16 * g + 8 : 16 * g + 16] for g in range(2)] + [total[:, 40:43]]
        wg_out[...] = jnp.concatenate(pieces + [total[:, 48:86]], 1)

    for d in range(1, n_lat):

        @when_upper(d)
        def _(d=d):
            lat_copy(d).wait_send()

    rows_all.wait_send()

    @pl.when(jnp.logical_not(top))
    def _():
        to_north.wait_send()
        to_nw.wait_send()

    @pl.when(top)
    def _():
        fold_all.wait_send()

    @pl.when(jnp.logical_not(bottom))
    def _():
        to_south.wait_send()
        to_se.wait_send()

    to_east.wait_send()
    to_west.wait_send()
    wp_copy.wait()

    @pl.loop(0, n8)
    def _(i):
        pltpu.make_async_copy(GR.at[i + 1], gr_out.at[i], gsem.at[i]).wait()


def feature_kernel(gr, wp, out, held, sems):
    pieces, ft = sems.shape[0], held.shape[1]
    per = held.shape[0] // pieces
    in_slot = gr.shape[2] // per
    copies = []
    for i in range(pieces):
        at = slice(i * per, (i + 1) * per)
        cells = slice(i % in_slot * per, (i % in_slot + 1) * per)
        held[at, :] = lax.dot_general(
            gr[i // in_slot, :, cells], wp[...], (((0,), (0,)), ((), ())),
            preferred_element_type=F32,
        ).astype(BF16)
        copies.append(pltpu.make_async_copy(held.at[at], out.at[at], sems.at[i]))
        copies[-1].start()
    for copy in copies:
        copy.wait()


def per_device(n_lon, n_lat, features, head_weight, target, metrics, masks, partner):
    R, C, ft = features.shape
    ch = target.shape[0]
    blk = ft // n_lon
    n8 = R // 8
    cells = R * C
    hbm = pl.BlockSpec(memory_space=pl.ANY)
    vmem = pl.BlockSpec(memory_space=pltpu.VMEM)
    V = pltpu.VMEM
    D = pltpu.SemaphoreType.DMA
    gr, wp, wg = pl.pallas_call(
        grads_kernel,
        out_shape=(
            jax.ShapeDtypeStruct((n8, CHP, 8 * C), BF16),
            jax.ShapeDtypeStruct((CHP, ft), BF16),
            jax.ShapeDtypeStruct((blk, ch), F32),
        ),
        in_specs=[pl.BlockSpec(memory_space=pltpu.HBM)] * 6,
        out_specs=(hbm, hbm, vmem),
        scratch_shapes=[
            V((R, C, ft), BF16),
            V((2, C, ft), BF16),
            V((2 * ROW, C), F32),
            V((ch + 4, R, C), BF16),
            V((R, 88, C), F32),
            V((6, R, C), F32),
            V((4, R, C), jnp.int32),
            V((ch, ft), BF16),
            V((n_lon, C), jnp.int32),
            V((CHP, ft), BF16),
            V(((R + 2) * ROW, C), F32),
            V((ROW, C), F32),
            V((2 * R, ft), BF16),
            V((ft, 2 * R), BF16),
            V((48, C), F32),
            V((ROW, C), F32),
            V((ROW, C), F32),
            V((32, C), F32),
            V((32, C), F32),
            V((24, C), F32),
            V((n_lon * 24, C), F32),
            V((n8 + 1, CHP, 8 * C), BF16),
            V((CHP, ft), F32),
            V((ft, C), F32),
            V((n_lon * blk, C), F32),
            V((n_lat, blk, C), F32),
            D((R // 16,)), D((4,)), D((6,)), D((n8,)), D((6,)), D((6,)),
            D, D, D, D, D((n_lat,)), D((n_lat,)),
        ],
        compiler_params=pltpu.CompilerParams(
            collective_id=0, has_side_effects=True, vmem_limit_bytes=48 * 1024 * 1024
        ),
        cost_estimate=pl.CostEstimate(
            flops=4 * cells * ft * CHP, bytes_accessed=12 * 1024 * 1024, transcendentals=0
        ),
        name="grads_and_weight_grad",
    )(
        *(
            pltpu.with_memory_space_constraint(x, pltpu.HBM)
            for x in (
                features, target, metrics, masks, head_weight.T,
                partner.reshape(n_lon, C),
            )
        )
    )
    feature_grad = pl.pallas_call(
        feature_kernel,
        out_shape=jax.ShapeDtypeStruct((cells, ft), BF16),
        in_specs=[vmem, vmem],
        out_specs=hbm,
        scratch_shapes=[V((cells, ft), BF16), D((2 * n8,))],
        compiler_params=pltpu.CompilerParams(vmem_limit_bytes=32 * 1024 * 1024),
        cost_estimate=pl.CostEstimate(
            flops=2 * cells * ft * CHP, bytes_accessed=10 * 1024 * 1024, transcendentals=0
        ),
        name="feature_grad",
    )(gr, wp)
    down = [(k, k - n_lat // 2) for k in range(n_lat // 2, n_lat)]
    weight_grad = wg + lax.ppermute(wg, "lat", down)
    return feature_grad.reshape(R, C, ft), weight_grad


def solution(mesh):
    return jax.shard_map(
        functools.partial(per_device, mesh.shape["lon"], mesh.shape["lat"]),
        mesh=mesh,
        in_specs=(
            P("lat", "lon", None),
            P(),
            P(None, "lat", "lon"),
            P(None, "lat", "lon"),
            P(None, "lat", "lon"),
            P(),
        ),
        out_specs=(P("lat", "lon", None), P("lon", None)),
        check_vma=False,
    )
```

```python
import functools

import jax
import jax.numpy as jnp
from jax import lax
from jax.experimental import pallas as pl
from jax.experimental.pallas import tpu as pltpu
from jax.sharding import PartitionSpec as P

LEV = 19
CHP = 96
ROW = 56
MESH = pl.DeviceIdType.MESH
F32 = jnp.float32
BF16 = jnp.bfloat16
NT = (((1,), (1,)), ((), ()))
NN = (((1,), (0,)), ((), ()))


def lanes(shape):
    return lax.broadcasted_iota(jnp.int32, shape, len(shape) - 1)


def grads_kernel(
    feat, tgt, met, msk, wt, part, gr_out, wp_out, wg_out,
    F, FR, RS, Tb, Tf, M, K, Wv, Pv, Wp, EG, ED, FE, FT, DX, HW, HE, CNW, CSE, FS, FB, GR, ACC, WS, RB, LB,
    fsem, esem, lsem, gsem, hs, hr, fs_s, fs_r, rs_s, rs_r, ls_s, ls_r,
):
    n_lon, n_lat = lax.axis_size("lon"), lax.axis_size("lat")
    lon, lat = lax.axis_index("lon"), lax.axis_index("lat")
    R, C, ft = feat.shape
    n16 = R // 16
    n8 = R // 8
    blk = ft // n_lon
    top = lat == n_lat - 1
    bottom = lat == 0
    east = lax.rem(lon + 1, n_lon)
    west = lax.rem(lon + n_lon - 1, n_lon)
    up = lax.rem(lat + 1, n_lat)
    down = lax.rem(lat + n_lat - 1, n_lat)

    barrier = pltpu.get_barrier_semaphore()
    pl.semaphore_signal(barrier, inc=1, device_id=(east, lat), device_id_type=MESH)
    pl.semaphore_signal(barrier, inc=1, device_id=(west, lat), device_id_type=MESH)
    for d in range(1, n_lat):
        pl.semaphore_signal(
            barrier, inc=1, device_id=(lon, lax.rem(lat + d, n_lat)), device_id_type=MESH
        )
    pl.semaphore_signal(barrier, inc=1, device_id=(east, down), device_id_type=MESH)
    pl.semaphore_signal(barrier, inc=1, device_id=(west, up), device_id_type=MESH)

    def fcopy(c):
        at = (pl.ds(c * 16, 16), pl.ds(16, C - 32))
        return pltpu.make_async_copy(feat.at[at], F.at[at], fsem.at[c])

    def ecopy(k):
        at = (pl.ds(0, R), pl.ds(k * (C - 16), 16))
        return pltpu.make_async_copy(feat.at[at], F.at[at], esem.at[k])

    rows_in = [
        pltpu.make_async_copy(feat.at[0:1], FR.at[0:1], esem.at[2]),
        pltpu.make_async_copy(feat.at[R - 1 : R], FR.at[1:2], esem.at[3]),
    ]
    small = [
        pltpu.make_async_copy(met, M, lsem.at[0]),
        pltpu.make_async_copy(msk, K, lsem.at[1]),
        pltpu.make_async_copy(wt, Wv, lsem.at[2]),
        pltpu.make_async_copy(part, Pv, lsem.at[3]),
        pltpu.make_async_copy(tgt, Tb.at[0 : 4 * LEV], lsem.at[4]),
    ]
    for copy in small:
        copy.start()
    @pl.loop(2, n_lon - 1)
    def _(d):
        pl.semaphore_signal(
            barrier, inc=1, device_id=(lax.rem(lon + d, n_lon), lat), device_id_type=MESH
        )

    for copy in rows_in:
        copy.start()
    ecopy(0).start()
    ecopy(1).start()
    for i in range(n16):
        fcopy((i + n16 - 1) % n16).start()

    @pl.when(bottom)
    def _():
        EG[0:ROW, :] = jnp.zeros((ROW, C), F32)
        CSE[...] = jnp.zeros_like(CSE)

    @pl.when(top)
    def _():
        EG[(R + 1) * ROW : (R + 2) * ROW, :] = jnp.zeros((ROW, C), F32)
        CNW[...] = jnp.zeros_like(CNW)

    small[0].wait()
    small[1].wait()
    for g in range(n8):
        at = slice(8 * g, 8 * g + 8)
        um, vm = K[0, at, :].astype(F32), K[1, at, :].astype(F32)
        qm, hm = K[2, at, :].astype(F32), K[3, at, :].astype(F32)
        area_h = M[5, at, :]
        qw = 2.0 * qm / M[4, at, :]
        coefs = (
            M[0, at, :] * um, M[1, at, :] * um, M[3, at, :] * vm, M[2, at, :] * vm,
            qw, hm / area_h, area_h * hm, qw,
        )
        for k, value in enumerate(coefs):
            EG[pl.ds((8 * g + 1) * ROW + 24 + k, 8, stride=ROW), :] = value

    small[2].wait()
    p = lax.broadcasted_iota(jnp.int32, (CHP, 4 * LEV), 0)
    c = lax.broadcasted_iota(jnp.int32, (CHP, 4 * LEV), 1)
    level = (p // 16) * 8 + p % 8
    pick = (p < 48) & (level < LEV) & (c == level + LEV * ((p // 8) % 2))
    pick = pick | ((p >= 48) & (c == p - 10))
    wp = lax.dot_general(
        jnp.where(pick, 1.0, 0.0).astype(BF16), Wv[...], NN, preferred_element_type=F32
    )
    Wp[...] = wp.astype(BF16)
    wp_copy = pltpu.make_async_copy(Wp, wp_out, lsem.at[5])
    wp_copy.start()
    small[3].wait()

    firsts = [0, LEV, 8, LEV + 8, 16, LEV + 16] + [2 * LEV + 8 * k for k in range(5)]
    Tb[4 * LEV :, :, :] = jnp.zeros((4, R, C), BF16)
    small[4].wait()

    def widen(i, _):
        at = pl.ds(pl.multiple_of(16 * i, 16), 16)
        for k, ch in enumerate(firsts):
            turned = jnp.swapaxes(Tb[ch : ch + 8, at, :].astype(F32), 0, 1)
            Tf[at, 8 * k : 8 * k + 8, :] = turned
        return 0

    lax.fori_loop(0, n16, widen, 0)

    half8 = lanes((8, C)) >> 1

    def pack(i, packed):
        packed = list(packed)
        for j in range(16):
            r = 16 * i + j
            base = pl.multiple_of((r + 1) * ROW, 8)
            rows = [Tf[r, 8 * k : 8 * k + 8, :] for k in range(6)]
            rows.append(EG[pl.ds(base + 24, 8), :])
            by = 2 * r + 1
            packed = [
                jnp.where(half8 == r, pltpu.roll(x, by, 1), y) for x, y in zip(rows, packed)
            ]
        return tuple(packed)

    packed = lax.fori_loop(0, n16, pack, (jnp.zeros((8, C), F32),) * 7)
    for copy in rows_in:
        copy.wait()
    at_rows = lax.dot_general(
        Wp[0:48, :], FR[...].reshape(2 * C, ft), NT, preferred_element_type=F32
    )
    for k, r in enumerate((0, R - 1)):
        found = at_rows[:, k * C : (k + 1) * C] - Tf[r, 0:48, :]
        to = k * ROW
        for g in range(3):
            RS[to + 8 * g : to + 8 * g + 8, :] = found[16 * g : 16 * g + 8]
            RS[to + 32 + 8 * g : to + 40 + 8 * g, :] = found[16 * g + 8 : 16 * g + 16]
        RS[to + 24 : to + 32, :] = EG[(r + 1) * ROW + 24 : (r + 1) * ROW + 32, :]

    q = lax.broadcasted_iota(jnp.int32, (32, 512), 0)
    cell = lax.broadcasted_iota(jnp.int32, (32, 512), 1)
    wanted = (q >> 1) * 16 + jnp.where((q & 1) == 1, 0, 256 + 15)
    choose = jnp.where(cell == wanted, 1.0, 0.0).astype(BF16)
    ecopy(0).wait()
    ecopy(1).wait()
    for i in range(n16):
        rows = slice(16 * i, 16 * i + 16)
        sides = [F[rows, 0:16, :].reshape(256, ft), F[rows, C - 16 : C, :].reshape(256, ft)]
        FE[32 * i : 32 * i + 32, :] = jnp.dot(
            choose, jnp.concatenate(sides, 0), preferred_element_type=F32
        ).astype(BF16)
    at_edges = lax.dot_general(Wp[0:48, :], FE[...], NT, preferred_element_type=F32)
    ED[...] = jnp.zeros_like(ED)
    for k in range(6):
        to = 8 * (k // 2) + 32 * (k % 2)
        ED[to : to + 8, 0 : 2 * R] = at_edges[8 * k : 8 * k + 8] - packed[k][:, 0 : 2 * R]
    ED[24:32, :] = packed[6]

    def send(src, dst, k, device):
        return pltpu.make_async_remote_copy(
            src_ref=src, dst_ref=dst, send_sem=hs.at[k], recv_sem=hr.at[k],
            device_id=device, device_id_type=MESH,
        )

    south_row = EG.at[0:ROW]
    first_row = RS.at[0:ROW]
    last_row = RS.at[ROW : 2 * ROW]
    north_row = EG.at[(R + 1) * ROW : (R + 2) * ROW]
    to_north = send(last_row, south_row, 0, (lon, up))
    to_south = send(first_row, north_row, 1, (lon, down))
    to_east = send(ED, HW, 2, (east, lat))
    to_west = send(ED, HE, 3, (west, lat))
    to_nw = send(RS.at[ROW + 24 : 2 * ROW], CSE, 4, (west, up))
    to_se = send(RS.at[0:32], CNW, 5, (east, down))

    def fold_copy(peer):
        return pltpu.make_async_remote_copy(
            src_ref=FS, dst_ref=FB.at[pl.ds(pl.multiple_of(lon * 24, 8), 24)],
            send_sem=fs_s, recv_sem=fs_r, device_id=(peer, lat), device_id_type=MESH,
        )

    others = pl.ds(0, (n_lon - 1) * 24)
    fold_all = pltpu.make_async_remote_copy(
        src_ref=FB.at[others], dst_ref=FB.at[others], send_sem=fs_s, recv_sem=fs_r,
        device_id=(east, lat), device_id_type=MESH,
    )

    pl.semaphore_wait(barrier, n_lon + n_lat)

    @pl.when(jnp.logical_not(top))
    def _():
        to_nw.start()
        to_north.start()

    @pl.when(jnp.logical_not(bottom))
    def _():
        to_se.start()
        to_south.start()

    to_east.start()
    to_west.start()

    @pl.when(top)
    def _():
        flux = RS[ROW : ROW + 24, :] * RS[ROW + 24 : ROW + 25, :]
        sub = lax.broadcasted_iota(jnp.int32, (24, C), 0)
        FS[...] = jnp.where(sub == 23, RS[ROW + 28 : ROW + 29, :], flux)

        @pl.loop(1, n_lon)
        def _(d):
            fold_copy(lax.rem(lon + d, n_lon)).start()

        FB[pl.ds(pl.multiple_of(lon * 24, 8), 24), :] = FS[...]

    def errors_chunk(i, _):
        chunk = (i + n16 - 1) % n16
        r0 = chunk * 16
        fcopy(chunk).wait()
        for j4 in range(4):
            cells = F[pl.ds(r0 + 4 * j4, 4), :, :].reshape(4 * C, ft)
            predicted = lax.dot_general(Wp[...], cells, NT, preferred_element_type=F32)
            for j in range(4):
                q = 4 * j4 + j
                r = r0 + q
                base = (r + 1) * ROW
                mine = predicted[0:88, j * C : (j + 1) * C] - Tf[r]
                for k in range(3):
                    EG[pl.ds(base + 8 * k, 8), :] = mine[16 * k : 16 * k + 8]
                    EG[pl.ds(base + 32 + 8 * k, 8), :] = mine[16 * k + 8 : 16 * k + 16]
                other = mine[48:88] * EG[pl.ds(base + 30, 1), :]
                other = jnp.concatenate([other, jnp.zeros((8, C), F32)], 0)
                GR[2 * chunk + q // 8 + 1, 48:CHP, (q % 8) * C : (q % 8 + 1) * C] = other.astype(BF16)

        return 0

    for i in range(n16):
        errors_chunk(i, 0)

    def roll(x, by):
        return pltpu.roll(x, by, 1)

    def u_at(base, g):
        return EG[pl.ds(base + 8 * g, 8), :]

    def v_at(base, g):
        return EG[pl.ds(base + 32 + 8 * g, 8), :]

    def coef(base, k):
        return EG[pl.ds(base + 24 + k, 1), :]

    def west_of(x):
        return roll(x, 1)

    def east_of(x):
        return roll(x, C - 1)

    def state_at(r):
        b0, b1 = r * ROW, (r + 1) * ROW
        state = []
        for g in range(3):
            uf = u_at(b1, g) * coef(b1, 0)
            va = v_at(b1, g) * coef(b1, 3)
            ua = u_at(b1, g) * coef(b1, 1)
            before = v_at(b0, g) * coef(b0, 3)
            ct = coef(b1, 5) * (ua - west_of(ua) - va + before)
            df = coef(b0, 7) * (u_at(b0, g) * coef(b0, 0) - uf)
            state.append((uf, va, ct, df))
        return state

    ACC[...] = jnp.zeros_like(ACC)


    def weight_chunk(slot, chunk):
        cells = F[8 * chunk : 8 * chunk + 8, :, :].reshape(8 * C, ft)
        ACC[...] += jnp.dot(GR[slot], cells, preferred_element_type=F32)

    def stencil_chunk(i, carry, done):
        last = i == n8 - 1

        if last:
            @pl.when(jnp.logical_not(top))
            def _():
                to_south.wait_recv()

            @pl.when(top)
            def _():
                fold_all.wait_recv()

                wide = (24, C)
                mirror = Pv[pl.ds(lon, 1), :]
                which = jnp.broadcast_to(mirror >> 7, wide)
                within = jnp.broadcast_to(mirror & 127, wide)

                found = jnp.zeros(wide, F32)
                for b in range(n_lon):
                    there = jnp.take_along_axis(
                        FB[24 * b : 24 * b + 24, :], within, axis=1, mode="promise_in_bounds"
                    )
                    found = jnp.where(which == b, there, found)
                beyond = (R + 1) * ROW
                EG[beyond : beyond + 24, :] = -found
                EG[beyond + 24 : beyond + 25, :] = jnp.ones((1, C), F32)
                at = R * ROW + 31
                EG[at : at + 1, :] = EG[at : at + 1, :] + found[23:24]

        if done is not None:
            weight_chunk(done + 1, done)
        after = []
        for g in range(3):
            uf, va, ct, df = carry[g]
            for j in range(8):
                r = 8 * i + j
                b0 = (r + 1) * ROW
                b1 = (r + 2) * ROW
                u1, v1 = u_at(b1, g), v_at(b1, g)
                uf1, ua1, va1 = u1 * coef(b1, 0), u1 * coef(b1, 1), v1 * coef(b1, 3)
                df1 = coef(b0, 7) * (uf - uf1)
                ct1 = coef(b1, 5) * (ua1 - west_of(ua1) - va1 + va)
                vf = v_at(b0, g) * coef(b0, 2)
                summed = coef(b0, 4) * (east_of(vf) - vf)
                grad_v = west_of(summed) - summed
                grad_uy = ct - east_of(ct)
                gu = coef(b0, 0) * (df1 - df) + coef(b0, 1) * grad_uy
                gv = coef(b0, 2) * grad_v + coef(b0, 3) * (ct1 - ct)
                GR[i + 1, 16 * g : 16 * g + 16, j * C : (j + 1) * C] = jnp.concatenate(
                    [gu, gv], 0
                ).astype(BF16)
                uf, va, ct, df = uf1, va1, ct1, df1
            after.append((uf, va, ct, df))
        return tuple(after)

    carry, done = state_at(8), None
    for i in [*range(1, n8 - 1), 0, n8 - 1]:
        if i == 0:
            kept = carry

            @pl.when(jnp.logical_not(bottom))
            def _():
                to_north.wait_recv()

            carry = state_at(0)
        elif i == n8 - 1:
            carry = kept
        carry = stencil_chunk(i, carry, done)
        done = i
    weight_chunk(done + 1, done)

    lane = lanes((24, C))
    even = (lane & 1) == 0
    even_row = (lanes((ROW, C)) & 1) == 0
    ends = lane >= 2 * R - 2
    ed = ED[...]
    swap = jnp.where(even_row, roll(ed, C - 1), roll(ed, 1))

    def part(x, k):
        return x[24 + k : 25 + k]

    u_own, v_own = ed[0:24], ed[32:56]
    u_swap, v_swap = swap[0:24], swap[32:56]
    ua_own, ua_swap = u_own * part(ed, 1), u_swap * part(swap, 1)
    vf_own, vf_swap = v_own * part(ed, 2), v_swap * part(swap, 2)
    va_swap = v_swap * part(swap, 3)
    below = EG[32:56, :] * EG[27:28, :]
    ct_swap = part(swap, 5) * (ua_swap - ua_own - va_swap + jnp.where(lane == 0, below, roll(va_swap, 2)))
    flux_swap = part(swap, 4) * (vf_own - vf_swap)
    beyond = (R + 1) * ROW
    ua_up = EG[beyond : beyond + 24, :] * EG[beyond + 25 : beyond + 26, :]
    hw_up = jnp.broadcast_to(EG[beyond + 29 : beyond + 30, :], (24, C))

    scale = 1.0 / (R * n_lat * C * n_lon)
    acc = jnp.concatenate([ACC[...] * scale, jnp.zeros((C - CHP, ft), F32)], 0)
    WS[...] = acc.T
    FT[...] = FE[...].T

    to_east.wait_recv()
    to_west.wait_recv()

    @pl.when(jnp.logical_not(bottom))
    def _():
        to_nw.wait_recv()

    @pl.when(jnp.logical_not(top))
    def _():
        to_se.wait_recv()

    corner = CSE[8:32, :] * CSE[3:4, :]
    ua_far = CNW[0:24, :] * CNW[25:26, :]
    gap_top = roll(hw_up * roll(ua_up - ua_far, 1), 2 * R - 1)
    beside = jnp.where(even_row, roll(HE[...], C - 1), roll(HW[...], 1))
    u_side, v_side = beside[0:24], beside[32:56]
    ua_side, vf_side = u_side * part(beside, 1), v_side * part(beside, 2)
    va_side = v_side * part(beside, 3)
    va_side0 = jnp.where(lane == 0, corner, roll(va_side, 2))
    ct_side = part(beside, 5) * (ua_side - ua_own - va_side + va_side0)
    flux_e = part(ed, 4) * (vf_swap - vf_side)
    gap = part(ed, 5) * (ua_swap - ua_side)
    gap_up = jnp.where(ends, gap_top, roll(gap, C - 2))
    flux_w = part(beside, 4) * (vf_own - vf_side) - flux_swap
    fix_u = part(ed, 1) * jnp.where(even, ct_swap - ct_side, gap)
    fix_v = part(ed, 2) * jnp.where(even, flux_e, flux_w)
    fix_v = fix_v + jnp.where(even, 0.0, part(ed, 3) * (gap_up - gap))
    fix = []
    for g in range(3):
        fix += [fix_u[8 * g : 8 * g + 8], fix_v[8 * g : 8 * g + 8]]
    fix = jnp.concatenate(fix, 0)
    DX[...] = fix
    more = lax.dot_general(
        FT[...], fix[:, 0 : 2 * R].astype(BF16), NT, preferred_element_type=F32
    )
    WS[:, 0:48] += more * scale

    def rows_copy(peer):
        src = WS.at[pl.ds(pl.multiple_of(peer * blk, blk), blk)]
        dst = RB.at[pl.ds(pl.multiple_of(lon * blk, blk), blk)]
        return pltpu.make_async_remote_copy(
            src_ref=src, dst_ref=dst, send_sem=rs_s, recv_sem=rs_r,
            device_id=(peer, lat), device_id_type=MESH,
        )

    rows_all = pltpu.make_async_remote_copy(
        src_ref=WS.at[0 : (n_lon - 1) * blk], dst_ref=RB.at[0 : (n_lon - 1) * blk],
        send_sem=rs_s, recv_sem=rs_r, device_id=(east, lat), device_id_type=MESH,
    )

    @pl.loop(1, n_lon)
    def _(d):
        rows_copy(lax.rem(lon + d, n_lon)).start()

    @pl.loop(0, n8)
    def _(i):
        at_ends = lanes((48, C))
        at_ends = (at_ends == 0) | (at_ends == C - 1)
        for j in range(8):
            here = (i + 1, slice(0, 48), slice(j * C, (j + 1) * C))
            held = GR[here].astype(F32)
            more = roll(DX[...], C - 1 - 2 * (8 * i + j))
            GR[here] = jnp.where(at_ends, held + more, held).astype(BF16)
        pltpu.make_async_copy(GR.at[i + 1], gr_out.at[i], gsem.at[i]).start()

    here = pl.ds(pl.multiple_of(lon * blk, blk), blk)
    RB[here, :] = WS[here, :]

    rows_all.wait_recv()
    total = RB[0:blk, :]
    for k in range(1, n_lon):
        total = total + RB[k * blk : (k + 1) * blk, :]
    LB[lat] = total

    def lat_copy(d):
        return pltpu.make_async_remote_copy(
            src_ref=LB.at[lat], dst_ref=LB.at[lat], send_sem=ls_s.at[d], recv_sem=ls_r.at[d],
            device_id=(lon, lax.rem(lat + d, n_lat)), device_id_type=MESH,
        )

    def when_upper(d):
        return pl.when(lax.rem(lat + d, n_lat) >= n_lat // 2)

    for d in range(1, n_lat):

        @when_upper(d)
        def _(d=d):
            lat_copy(d).start()

    wg_out[...] = jnp.zeros_like(wg_out)

    @when_upper(0)
    def _():
        for d in range(1, n_lat):
            lat_copy(d).wait_recv()
        total = LB[0]
        for k in range(1, n_lat):
            total = total + LB[k]
        pieces = [total[:, 16 * g : 16 * g + 8] for g in range(2)] + [total[:, 32:35]]
        pieces += [total[:, 16 * g + 8 : 16 * g + 16] for g in range(2)] + [total[:, 40:43]]
        wg_out[...] = jnp.concatenate(pieces + [total[:, 48:86]], 1)

    for d in range(1, n_lat):

        @when_upper(d)
        def _(d=d):
            lat_copy(d).wait_send()

    rows_all.wait_send()

    @pl.when(jnp.logical_not(top))
    def _():
        to_north.wait_send()
        to_nw.wait_send()

    @pl.when(top)
    def _():
        fold_all.wait_send()

    @pl.when(jnp.logical_not(bottom))
    def _():
        to_south.wait_send()
        to_se.wait_send()

    to_east.wait_send()
    to_west.wait_send()
    wp_copy.wait()

    @pl.loop(0, n8)
    def _(i):
        pltpu.make_async_copy(GR.at[i + 1], gr_out.at[i], gsem.at[i]).wait()


def feature_kernel(gr, wp, out, held, sems):
    pieces, ft = sems.shape[0], held.shape[1]
    per = held.shape[0] // pieces
    in_slot = gr.shape[2] // per
    copies = []
    for i in range(pieces):
        at = slice(i * per, (i + 1) * per)
        cells = slice(i % in_slot * per, (i % in_slot + 1) * per)
        held[at, :] = lax.dot_general(
            gr[i // in_slot, :, cells], wp[...], (((0,), (0,)), ((), ())),
            preferred_element_type=F32,
        ).astype(BF16)
        copies.append(pltpu.make_async_copy(held.at[at], out.at[at], sems.at[i]))
        copies[-1].start()
    for copy in copies:
        copy.wait()


def per_device(n_lon, n_lat, features, head_weight, target, metrics, masks, partner):
    R, C, ft = features.shape
    ch = target.shape[0]
    blk = ft // n_lon
    n8 = R // 8
    cells = R * C
    hbm = pl.BlockSpec(memory_space=pl.ANY)
    vmem = pl.BlockSpec(memory_space=pltpu.VMEM)
    V = pltpu.VMEM
    D = pltpu.SemaphoreType.DMA
    gr, wp, wg = pl.pallas_call(
        grads_kernel,
        out_shape=(
            jax.ShapeDtypeStruct((n8, CHP, 8 * C), BF16),
            jax.ShapeDtypeStruct((CHP, ft), BF16),
            jax.ShapeDtypeStruct((blk, ch), F32),
        ),
        in_specs=[pl.BlockSpec(memory_space=pltpu.HBM)] * 6,
        out_specs=(hbm, hbm, vmem),
        scratch_shapes=[
            V((R, C, ft), BF16),
            V((2, C, ft), BF16),
            V((2 * ROW, C), F32),
            V((ch + 4, R, C), BF16),
            V((R, 88, C), F32),
            V((6, R, C), F32),
            V((4, R, C), jnp.int32),
            V((ch, ft), BF16),
            V((n_lon, C), jnp.int32),
            V((CHP, ft), BF16),
            V(((R + 2) * ROW, C), F32),
            V((ROW, C), F32),
            V((2 * R, ft), BF16),
            V((ft, 2 * R), BF16),
            V((48, C), F32),
            V((ROW, C), F32),
            V((ROW, C), F32),
            V((32, C), F32),
            V((32, C), F32),
            V((24, C), F32),
            V((n_lon * 24, C), F32),
            V((n8 + 1, CHP, 8 * C), BF16),
            V((CHP, ft), F32),
            V((ft, C), F32),
            V((n_lon * blk, C), F32),
            V((n_lat, blk, C), F32),
            D((R // 16,)), D((4,)), D((6,)), D((n8,)), D((6,)), D((6,)),
            D, D, D, D, D((n_lat,)), D((n_lat,)),
        ],
        compiler_params=pltpu.CompilerParams(
            collective_id=0, has_side_effects=True, vmem_limit_bytes=48 * 1024 * 1024
        ),
        cost_estimate=pl.CostEstimate(
            flops=4 * cells * ft * CHP, bytes_accessed=12 * 1024 * 1024, transcendentals=0
        ),
        name="grads_and_weight_grad",
    )(
        *(
            pltpu.with_memory_space_constraint(x, pltpu.HBM)
            for x in (
                features, target, metrics, masks, head_weight.T,
                partner.reshape(n_lon, C),
            )
        )
    )
    feature_grad = pl.pallas_call(
        feature_kernel,
        out_shape=jax.ShapeDtypeStruct((cells, ft), BF16),
        in_specs=[vmem, vmem],
        out_specs=hbm,
        scratch_shapes=[V((cells, ft), BF16), D((2 * n8,))],
        compiler_params=pltpu.CompilerParams(vmem_limit_bytes=32 * 1024 * 1024),
        cost_estimate=pl.CostEstimate(
            flops=2 * cells * ft * CHP, bytes_accessed=10 * 1024 * 1024, transcendentals=0
        ),
        name="feature_grad",
    )(gr, wp)
    down = [(k, k - n_lat // 2) for k in range(n_lat // 2, n_lat)]
    weight_grad = wg + lax.ppermute(wg, "lat", down)
    return feature_grad.reshape(R, C, ft), weight_grad


def solution(mesh):
    return jax.shard_map(
        functools.partial(per_device, mesh.shape["lon"], mesh.shape["lat"]),
        mesh=mesh,
        in_specs=(
            P("lat", "lon", None),
            P(),
            P(None, "lat", "lon"),
            P(None, "lat", "lon"),
            P(None, "lat", "lon"),
            P(),
        ),
        out_specs=(P("lat", "lon", None), P("lon", None)),
        check_vma=False,
    )
```

```python
import functools

import jax
import jax.numpy as jnp
from jax import lax
from jax.experimental import pallas as pl
from jax.experimental.pallas import tpu as pltpu
from jax.sharding import PartitionSpec as P

LEV = 19
CHP = 96
ROW = 56
MESH = pl.DeviceIdType.MESH
F32 = jnp.float32
BF16 = jnp.bfloat16
NT = (((1,), (1,)), ((), ()))
NN = (((1,), (0,)), ((), ()))


def lanes(shape):
    return lax.broadcasted_iota(jnp.int32, shape, len(shape) - 1)


def grads_kernel(
    feat, tgt, met, msk, wt, part, gr_out, wp_out, wg_out,
    F, FR, RS, Tb, Tf, M, K, Wv, Pv, Wp, EG, ED, FE, FT, DX, HW, HE, CNW, CSE, FS, FB, GR, ACC, WS, RB, LB,
    fsem, esem, lsem, gsem, hs, hr, fs_s, fs_r, rs_s, rs_r, ls_s, ls_r,
):
    n_lon, n_lat = lax.axis_size("lon"), lax.axis_size("lat")
    lon, lat = lax.axis_index("lon"), lax.axis_index("lat")
    R, C, ft = feat.shape
    n16 = R // 16
    n8 = R // 8
    blk = ft // n_lon
    top = lat == n_lat - 1
    bottom = lat == 0
    east = lax.rem(lon + 1, n_lon)
    west = lax.rem(lon + n_lon - 1, n_lon)
    up = lax.rem(lat + 1, n_lat)
    down = lax.rem(lat + n_lat - 1, n_lat)

    barrier = pltpu.get_barrier_semaphore()
    pl.semaphore_signal(barrier, inc=1, device_id=(east, lat), device_id_type=MESH)
    pl.semaphore_signal(barrier, inc=1, device_id=(west, lat), device_id_type=MESH)
    for d in range(1, n_lat):
        pl.semaphore_signal(
            barrier, inc=1, device_id=(lon, lax.rem(lat + d, n_lat)), device_id_type=MESH
        )
    pl.semaphore_signal(barrier, inc=1, device_id=(east, down), device_id_type=MESH)
    pl.semaphore_signal(barrier, inc=1, device_id=(west, up), device_id_type=MESH)

    def fcopy(c):
        at = (pl.ds(c * 16, 16), pl.ds(16, C - 32))
        return pltpu.make_async_copy(feat.at[at], F.at[at], fsem.at[c])

    def ecopy(k):
        at = (pl.ds(0, R), pl.ds(k * (C - 16), 16))
        return pltpu.make_async_copy(feat.at[at], F.at[at], esem.at[k])

    rows_in = [
        pltpu.make_async_copy(feat.at[0:1], FR.at[0:1], esem.at[2]),
        pltpu.make_async_copy(feat.at[R - 1 : R], FR.at[1:2], esem.at[3]),
    ]
    small = [
        pltpu.make_async_copy(met, M, lsem.at[0]),
        pltpu.make_async_copy(msk, K, lsem.at[1]),
        pltpu.make_async_copy(wt, Wv, lsem.at[2]),
        pltpu.make_async_copy(part, Pv, lsem.at[3]),
        pltpu.make_async_copy(tgt, Tb.at[0 : 4 * LEV], lsem.at[4]),
    ]
    for copy in small:
        copy.start()
    for d in range(2, n_lon - 1):
        pl.semaphore_signal(
            barrier, inc=1, device_id=(lax.rem(lon + d, n_lon), lat), device_id_type=MESH
        )

    for copy in rows_in:
        copy.start()
    ecopy(0).start()
    ecopy(1).start()
    for i in range(n16):
        fcopy((i + n16 - 1) % n16).start()

    @pl.when(bottom)
    def _():
        EG[0:ROW, :] = jnp.zeros((ROW, C), F32)
        CSE[...] = jnp.zeros_like(CSE)

    @pl.when(top)
    def _():
        EG[(R + 1) * ROW : (R + 2) * ROW, :] = jnp.zeros((ROW, C), F32)
        CNW[...] = jnp.zeros_like(CNW)

    small[0].wait()
    small[1].wait()
    for g in range(n8):
        at = slice(8 * g, 8 * g + 8)
        um, vm = K[0, at, :].astype(F32), K[1, at, :].astype(F32)
        qm, hm = K[2, at, :].astype(F32), K[3, at, :].astype(F32)
        area_h = M[5, at, :]
        qw = 2.0 * qm / M[4, at, :]
        coefs = (
            M[0, at, :] * um, M[1, at, :] * um, M[3, at, :] * vm, M[2, at, :] * vm,
            qw, hm / area_h, area_h * hm, qw,
        )
        for k, value in enumerate(coefs):
            EG[pl.ds((8 * g + 1) * ROW + 24 + k, 8, stride=ROW), :] = value

    small[2].wait()
    p = lax.broadcasted_iota(jnp.int32, (CHP, 4 * LEV), 0)
    c = lax.broadcasted_iota(jnp.int32, (CHP, 4 * LEV), 1)
    level = (p // 16) * 8 + p % 8
    pick = (p < 48) & (level < LEV) & (c == level + LEV * ((p // 8) % 2))
    pick = pick | ((p >= 48) & (c == p - 10))
    wp = lax.dot_general(
        jnp.where(pick, 1.0, 0.0).astype(BF16), Wv[...], NN, preferred_element_type=F32
    )
    Wp[...] = wp.astype(BF16)
    wp_copy = pltpu.make_async_copy(Wp, wp_out, lsem.at[5])
    wp_copy.start()
    small[3].wait()

    firsts = [0, LEV, 8, LEV + 8, 16, LEV + 16] + [2 * LEV + 8 * k for k in range(5)]
    Tb[4 * LEV :, :, :] = jnp.zeros((4, R, C), BF16)
    small[4].wait()

    def widen(i, _):
        at = pl.ds(pl.multiple_of(16 * i, 16), 16)
        for k, ch in enumerate(firsts):
            turned = jnp.swapaxes(Tb[ch : ch + 8, at, :].astype(F32), 0, 1)
            Tf[at, 8 * k : 8 * k + 8, :] = turned
        return 0

    lax.fori_loop(0, n16, widen, 0)

    half8 = lanes((8, C)) >> 1

    def pack(i, packed):
        packed = list(packed)
        for j in range(16):
            r = 16 * i + j
            base = pl.multiple_of((r + 1) * ROW, 8)
            rows = [Tf[r, 8 * k : 8 * k + 8, :] for k in range(6)]
            rows.append(EG[pl.ds(base + 24, 8), :])
            by = 2 * r + 1
            packed = [
                jnp.where(half8 == r, pltpu.roll(x, by, 1), y) for x, y in zip(rows, packed)
            ]
        return tuple(packed)

    packed = lax.fori_loop(0, n16, pack, (jnp.zeros((8, C), F32),) * 7)
    for copy in rows_in:
        copy.wait()
    at_rows = lax.dot_general(
        Wp[0:48, :], FR[...].reshape(2 * C, ft), NT, preferred_element_type=F32
    )
    for k, r in enumerate((0, R - 1)):
        found = at_rows[:, k * C : (k + 1) * C] - Tf[r, 0:48, :]
        to = k * ROW
        for g in range(3):
            RS[to + 8 * g : to + 8 * g + 8, :] = found[16 * g : 16 * g + 8]
            RS[to + 32 + 8 * g : to + 40 + 8 * g, :] = found[16 * g + 8 : 16 * g + 16]
        RS[to + 24 : to + 32, :] = EG[(r + 1) * ROW + 24 : (r + 1) * ROW + 32, :]

    q = lax.broadcasted_iota(jnp.int32, (32, 512), 0)
    cell = lax.broadcasted_iota(jnp.int32, (32, 512), 1)
    wanted = (q >> 1) * 16 + jnp.where((q & 1) == 1, 0, 256 + 15)
    choose = jnp.where(cell == wanted, 1.0, 0.0).astype(BF16)
    ecopy(0).wait()
    ecopy(1).wait()
    for i in range(n16):
        rows = slice(16 * i, 16 * i + 16)
        sides = [F[rows, 0:16, :].reshape(256, ft), F[rows, C - 16 : C, :].reshape(256, ft)]
        FE[32 * i : 32 * i + 32, :] = jnp.dot(
            choose, jnp.concatenate(sides, 0), preferred_element_type=F32
        ).astype(BF16)
    at_edges = lax.dot_general(Wp[0:48, :], FE[...], NT, preferred_element_type=F32)
    ED[...] = jnp.zeros_like(ED)
    for k in range(6):
        to = 8 * (k // 2) + 32 * (k % 2)
        ED[to : to + 8, 0 : 2 * R] = at_edges[8 * k : 8 * k + 8] - packed[k][:, 0 : 2 * R]
    ED[24:32, :] = packed[6]

    def send(src, dst, k, device):
        return pltpu.make_async_remote_copy(
            src_ref=src, dst_ref=dst, send_sem=hs.at[k], recv_sem=hr.at[k],
            device_id=device, device_id_type=MESH,
        )

    south_row = EG.at[0:ROW]
    first_row = RS.at[0:ROW]
    last_row = RS.at[ROW : 2 * ROW]
    north_row = EG.at[(R + 1) * ROW : (R + 2) * ROW]
    to_north = send(last_row, south_row, 0, (lon, up))
    to_south = send(first_row, north_row, 1, (lon, down))
    to_east = send(ED, HW, 2, (east, lat))
    to_west = send(ED, HE, 3, (west, lat))
    to_nw = send(RS.at[ROW + 24 : 2 * ROW], CSE, 4, (west, up))
    to_se = send(RS.at[0:32], CNW, 5, (east, down))

    def fold_copy(peer):
        return pltpu.make_async_remote_copy(
            src_ref=FS, dst_ref=FB.at[pl.ds(pl.multiple_of(lon * 24, 8), 24)],
            send_sem=fs_s, recv_sem=fs_r, device_id=(peer, lat), device_id_type=MESH,
        )

    others = pl.ds(0, (n_lon - 1) * 24)
    fold_all = pltpu.make_async_remote_copy(
        src_ref=FB.at[others], dst_ref=FB.at[others], send_sem=fs_s, recv_sem=fs_r,
        device_id=(east, lat), device_id_type=MESH,
    )

    pl.semaphore_wait(barrier, n_lon + n_lat)

    @pl.when(jnp.logical_not(top))
    def _():
        to_nw.start()
        to_north.start()

    @pl.when(jnp.logical_not(bottom))
    def _():
        to_se.start()
        to_south.start()

    to_east.start()
    to_west.start()

    @pl.when(top)
    def _():
        flux = RS[ROW : ROW + 24, :] * RS[ROW + 24 : ROW + 25, :]
        sub = lax.broadcasted_iota(jnp.int32, (24, C), 0)
        FS[...] = jnp.where(sub == 23, RS[ROW + 28 : ROW + 29, :], flux)

        @pl.loop(1, n_lon)
        def _(d):
            fold_copy(lax.rem(lon + d, n_lon)).start()

        FB[pl.ds(pl.multiple_of(lon * 24, 8), 24), :] = FS[...]

    def errors_chunk(i, _):
        chunk = (i + n16 - 1) % n16
        r0 = chunk * 16
        fcopy(chunk).wait()
        for j4 in range(4):
            cells = F[pl.ds(r0 + 4 * j4, 4), :, :].reshape(4 * C, ft)
            predicted = lax.dot_general(Wp[...], cells, NT, preferred_element_type=F32)
            for j in range(4):
                q = 4 * j4 + j
                r = r0 + q
                base = (r + 1) * ROW
                mine = predicted[0:88, j * C : (j + 1) * C] - Tf[r]
                for k in range(3):
                    EG[pl.ds(base + 8 * k, 8), :] = mine[16 * k : 16 * k + 8]
                    EG[pl.ds(base + 32 + 8 * k, 8), :] = mine[16 * k + 8 : 16 * k + 16]
                other = mine[48:88] * EG[pl.ds(base + 30, 1), :]
                other = jnp.concatenate([other, jnp.zeros((8, C), F32)], 0)
                GR[2 * chunk + q // 8 + 1, 48:CHP, (q % 8) * C : (q % 8 + 1) * C] = other.astype(BF16)

        return 0

    for i in range(n16):
        errors_chunk(i, 0)

    def roll(x, by):
        return pltpu.roll(x, by, 1)

    def u_at(base, g):
        return EG[pl.ds(base + 8 * g, 8), :]

    def v_at(base, g):
        return EG[pl.ds(base + 32 + 8 * g, 8), :]

    def coef(base, k):
        return EG[pl.ds(base + 24 + k, 1), :]

    def west_of(x):
        return roll(x, 1)

    def east_of(x):
        return roll(x, C - 1)

    def state_at(r):
        b0, b1 = r * ROW, (r + 1) * ROW
        state = []
        for g in range(3):
            uf = u_at(b1, g) * coef(b1, 0)
            va = v_at(b1, g) * coef(b1, 3)
            ua = u_at(b1, g) * coef(b1, 1)
            before = v_at(b0, g) * coef(b0, 3)
            ct = coef(b1, 5) * (ua - west_of(ua) - va + before)
            df = coef(b0, 7) * (u_at(b0, g) * coef(b0, 0) - uf)
            state.append((uf, va, ct, df))
        return state

    ACC[...] = jnp.zeros_like(ACC)


    def weight_chunk(slot, chunk):
        cells = F[8 * chunk : 8 * chunk + 8, :, :].reshape(8 * C, ft)
        ACC[...] += jnp.dot(GR[slot], cells, preferred_element_type=F32)

    def stencil_chunk(i, carry, done):
        last = i == n8 - 1

        if last:
            @pl.when(jnp.logical_not(top))
            def _():
                to_south.wait_recv()

            @pl.when(top)
            def _():
                fold_all.wait_recv()

                wide = (24, C)
                mirror = Pv[pl.ds(lon, 1), :]
                which = jnp.broadcast_to(mirror >> 7, wide)
                within = jnp.broadcast_to(mirror & 127, wide)

                found = jnp.zeros(wide, F32)
                for b in range(n_lon):
                    there = jnp.take_along_axis(
                        FB[24 * b : 24 * b + 24, :], within, axis=1, mode="promise_in_bounds"
                    )
                    found = jnp.where(which == b, there, found)
                beyond = (R + 1) * ROW
                EG[beyond : beyond + 24, :] = -found
                EG[beyond + 24 : beyond + 25, :] = jnp.ones((1, C), F32)
                at = R * ROW + 31
                EG[at : at + 1, :] = EG[at : at + 1, :] + found[23:24]

        if done is not None:
            weight_chunk(done + 1, done)
        after = []
        for g in range(3):
            uf, va, ct, df = carry[g]
            for j in range(8):
                r = 8 * i + j
                b0 = (r + 1) * ROW
                b1 = (r + 2) * ROW
                u1, v1 = u_at(b1, g), v_at(b1, g)
                uf1, ua1, va1 = u1 * coef(b1, 0), u1 * coef(b1, 1), v1 * coef(b1, 3)
                df1 = coef(b0, 7) * (uf - uf1)
                ct1 = coef(b1, 5) * (ua1 - west_of(ua1) - va1 + va)
                vf = v_at(b0, g) * coef(b0, 2)
                summed = coef(b0, 4) * (east_of(vf) - vf)
                grad_v = west_of(summed) - summed
                grad_uy = ct - east_of(ct)
                gu = coef(b0, 0) * (df1 - df) + coef(b0, 1) * grad_uy
                gv = coef(b0, 2) * grad_v + coef(b0, 3) * (ct1 - ct)
                GR[i + 1, 16 * g : 16 * g + 16, j * C : (j + 1) * C] = jnp.concatenate(
                    [gu, gv], 0
                ).astype(BF16)
                uf, va, ct, df = uf1, va1, ct1, df1
            after.append((uf, va, ct, df))
        return tuple(after)

    carry, done = state_at(8), None
    for i in [*range(1, n8 - 1), 0, n8 - 1]:
        if i == 0:
            kept = carry

            @pl.when(jnp.logical_not(bottom))
            def _():
                to_north.wait_recv()

            carry = state_at(0)
        elif i == n8 - 1:
            carry = kept
        carry = stencil_chunk(i, carry, done)
        done = i
    weight_chunk(done + 1, done)

    lane = lanes((24, C))
    even = (lane & 1) == 0
    even_row = (lanes((ROW, C)) & 1) == 0
    ends = lane >= 2 * R - 2
    ed = ED[...]
    swap = jnp.where(even_row, roll(ed, C - 1), roll(ed, 1))

    def part(x, k):
        return x[24 + k : 25 + k]

    u_own, v_own = ed[0:24], ed[32:56]
    u_swap, v_swap = swap[0:24], swap[32:56]
    ua_own, ua_swap = u_own * part(ed, 1), u_swap * part(swap, 1)
    vf_own, vf_swap = v_own * part(ed, 2), v_swap * part(swap, 2)
    va_swap = v_swap * part(swap, 3)
    below = EG[32:56, :] * EG[27:28, :]
    ct_swap = part(swap, 5) * (ua_swap - ua_own - va_swap + jnp.where(lane == 0, below, roll(va_swap, 2)))
    flux_swap = part(swap, 4) * (vf_own - vf_swap)
    beyond = (R + 1) * ROW
    ua_up = EG[beyond : beyond + 24, :] * EG[beyond + 25 : beyond + 26, :]
    hw_up = jnp.broadcast_to(EG[beyond + 29 : beyond + 30, :], (24, C))

    scale = 1.0 / (R * n_lat * C * n_lon)
    acc = jnp.concatenate([ACC[...] * scale, jnp.zeros((C - CHP, ft), F32)], 0)
    WS[...] = acc.T
    FT[...] = FE[...].T

    to_east.wait_recv()
    to_west.wait_recv()

    @pl.when(jnp.logical_not(bottom))
    def _():
        to_nw.wait_recv()

    @pl.when(jnp.logical_not(top))
    def _():
        to_se.wait_recv()

    corner = CSE[8:32, :] * CSE[3:4, :]
    ua_far = CNW[0:24, :] * CNW[25:26, :]
    gap_top = roll(hw_up * roll(ua_up - ua_far, 1), 2 * R - 1)
    beside = jnp.where(even_row, roll(HE[...], C - 1), roll(HW[...], 1))
    u_side, v_side = beside[0:24], beside[32:56]
    ua_side, vf_side = u_side * part(beside, 1), v_side * part(beside, 2)
    va_side = v_side * part(beside, 3)
    va_side0 = jnp.where(lane == 0, corner, roll(va_side, 2))
    ct_side = part(beside, 5) * (ua_side - ua_own - va_side + va_side0)
    flux_e = part(ed, 4) * (vf_swap - vf_side)
    gap = part(ed, 5) * (ua_swap - ua_side)
    gap_up = jnp.where(ends, gap_top, roll(gap, C - 2))
    flux_w = part(beside, 4) * (vf_own - vf_side) - flux_swap
    fix_u = part(ed, 1) * jnp.where(even, ct_swap - ct_side, gap)
    fix_v = part(ed, 2) * jnp.where(even, flux_e, flux_w)
    fix_v = fix_v + jnp.where(even, 0.0, part(ed, 3) * (gap_up - gap))
    fix = []
    for g in range(3):
        fix += [fix_u[8 * g : 8 * g + 8], fix_v[8 * g : 8 * g + 8]]
    fix = jnp.concatenate(fix, 0)
    DX[...] = fix
    more = lax.dot_general(
        FT[...], fix[:, 0 : 2 * R].astype(BF16), NT, preferred_element_type=F32
    )
    WS[:, 0:48] += more * scale

    def rows_copy(peer):
        src = WS.at[pl.ds(pl.multiple_of(peer * blk, blk), blk)]
        dst = RB.at[pl.ds(pl.multiple_of(lon * blk, blk), blk)]
        return pltpu.make_async_remote_copy(
            src_ref=src, dst_ref=dst, send_sem=rs_s, recv_sem=rs_r,
            device_id=(peer, lat), device_id_type=MESH,
        )

    rows_all = pltpu.make_async_remote_copy(
        src_ref=WS.at[0 : (n_lon - 1) * blk], dst_ref=RB.at[0 : (n_lon - 1) * blk],
        send_sem=rs_s, recv_sem=rs_r, device_id=(east, lat), device_id_type=MESH,
    )

    @pl.loop(1, n_lon)
    def _(d):
        rows_copy(lax.rem(lon + d, n_lon)).start()

    @pl.loop(0, n8)
    def _(i):
        at_ends = lanes((48, C))
        at_ends = (at_ends == 0) | (at_ends == C - 1)
        for j in range(8):
            here = (i + 1, slice(0, 48), slice(j * C, (j + 1) * C))
            held = GR[here].astype(F32)
            more = roll(DX[...], C - 1 - 2 * (8 * i + j))
            GR[here] = jnp.where(at_ends, held + more, held).astype(BF16)
        pltpu.make_async_copy(GR.at[i + 1], gr_out.at[i], gsem.at[i]).start()

    here = pl.ds(pl.multiple_of(lon * blk, blk), blk)
    RB[here, :] = WS[here, :]

    rows_all.wait_recv()
    total = RB[0:blk, :]
    for k in range(1, n_lon):
        total = total + RB[k * blk : (k + 1) * blk, :]
    LB[lat] = total

    def lat_copy(d):
        return pltpu.make_async_remote_copy(
            src_ref=LB.at[lat], dst_ref=LB.at[lat], send_sem=ls_s.at[d], recv_sem=ls_r.at[d],
            device_id=(lon, lax.rem(lat + d, n_lat)), device_id_type=MESH,
        )

    def when_upper(d):
        return pl.when(lax.rem(lat + d, n_lat) >= n_lat // 2)

    for d in range(1, n_lat):

        @when_upper(d)
        def _(d=d):
            lat_copy(d).start()

    wg_out[...] = jnp.zeros_like(wg_out)

    @when_upper(0)
    def _():
        for d in range(1, n_lat):
            lat_copy(d).wait_recv()
        total = LB[0]
        for k in range(1, n_lat):
            total = total + LB[k]
        pieces = [total[:, 16 * g : 16 * g + 8] for g in range(2)] + [total[:, 32:35]]
        pieces += [total[:, 16 * g + 8 : 16 * g + 16] for g in range(2)] + [total[:, 40:43]]
        wg_out[...] = jnp.concatenate(pieces + [total[:, 48:86]], 1)

    for d in range(1, n_lat):

        @when_upper(d)
        def _(d=d):
            lat_copy(d).wait_send()

    rows_all.wait_send()

    @pl.when(jnp.logical_not(top))
    def _():
        to_north.wait_send()
        to_nw.wait_send()

    @pl.when(top)
    def _():
        fold_all.wait_send()

    @pl.when(jnp.logical_not(bottom))
    def _():
        to_south.wait_send()
        to_se.wait_send()

    to_east.wait_send()
    to_west.wait_send()
    wp_copy.wait()

    @pl.loop(0, n8)
    def _(i):
        pltpu.make_async_copy(GR.at[i + 1], gr_out.at[i], gsem.at[i]).wait()


def feature_kernel(gr, wp, out, held, sems):
    pieces, ft = sems.shape[0], held.shape[1]
    per = held.shape[0] // pieces
    in_slot = gr.shape[2] // per
    copies = []
    for i in range(pieces):
        at = slice(i * per, (i + 1) * per)
        cells = slice(i % in_slot * per, (i % in_slot + 1) * per)
        held[at, :] = lax.dot_general(
            gr[i // in_slot, :, cells], wp[...], (((0,), (0,)), ((), ())),
            preferred_element_type=F32,
        ).astype(BF16)
        copies.append(pltpu.make_async_copy(held.at[at], out.at[at], sems.at[i]))
        copies[-1].start()
    for copy in copies:
        copy.wait()


def per_device(n_lon, n_lat, features, head_weight, target, metrics, masks, partner):
    R, C, ft = features.shape
    ch = target.shape[0]
    blk = ft // n_lon
    n8 = R // 8
    cells = R * C
    hbm = pl.BlockSpec(memory_space=pl.ANY)
    vmem = pl.BlockSpec(memory_space=pltpu.VMEM)
    V = pltpu.VMEM
    D = pltpu.SemaphoreType.DMA
    gr, wp, wg = pl.pallas_call(
        grads_kernel,
        out_shape=(
            jax.ShapeDtypeStruct((n8, CHP, 8 * C), BF16),
            jax.ShapeDtypeStruct((CHP, ft), BF16),
            jax.ShapeDtypeStruct((blk, ch), F32),
        ),
        in_specs=[pl.BlockSpec(memory_space=pltpu.HBM)] * 6,
        out_specs=(hbm, hbm, vmem),
        scratch_shapes=[
            V((R, C, ft), BF16),
            V((2, C, ft), BF16),
            V((2 * ROW, C), F32),
            V((ch + 4, R, C), BF16),
            V((R, 88, C), F32),
            V((6, R, C), F32),
            V((4, R, C), jnp.int32),
            V((ch, ft), BF16),
            V((n_lon, C), jnp.int32),
            V((CHP, ft), BF16),
            V(((R + 2) * ROW, C), F32),
            V((ROW, C), F32),
            V((2 * R, ft), BF16),
            V((ft, 2 * R), BF16),
            V((48, C), F32),
            V((ROW, C), F32),
            V((ROW, C), F32),
            V((32, C), F32),
            V((32, C), F32),
            V((24, C), F32),
            V((n_lon * 24, C), F32),
            V((n8 + 1, CHP, 8 * C), BF16),
            V((CHP, ft), F32),
            V((ft, C), F32),
            V((n_lon * blk, C), F32),
            V((n_lat, blk, C), F32),
            D((R // 16,)), D((4,)), D((6,)), D((n8,)), D((6,)), D((6,)),
            D, D, D, D, D((n_lat,)), D((n_lat,)),
        ],
        compiler_params=pltpu.CompilerParams(
            collective_id=0, has_side_effects=True, vmem_limit_bytes=48 * 1024 * 1024
        ),
        cost_estimate=pl.CostEstimate(
            flops=4 * cells * ft * CHP, bytes_accessed=12 * 1024 * 1024, transcendentals=0
        ),
        name="grads_and_weight_grad",
    )(
        *(
            pltpu.with_memory_space_constraint(x, pltpu.HBM)
            for x in (
                features, target, metrics, masks, head_weight.T,
                partner.reshape(n_lon, C),
            )
        )
    )
    feature_grad = pl.pallas_call(
        feature_kernel,
        out_shape=jax.ShapeDtypeStruct((cells, ft), BF16),
        in_specs=[vmem, vmem],
        out_specs=hbm,
        scratch_shapes=[V((cells, ft), BF16), D((2 * n8,))],
        compiler_params=pltpu.CompilerParams(vmem_limit_bytes=32 * 1024 * 1024),
        cost_estimate=pl.CostEstimate(
            flops=2 * cells * ft * CHP, bytes_accessed=10 * 1024 * 1024, transcendentals=0
        ),
        name="feature_grad",
    )(gr, wp)
    down = [(k, k - n_lat // 2) for k in range(n_lat // 2, n_lat)]
    weight_grad = wg + lax.ppermute(wg, "lat", down)
    return feature_grad.reshape(R, C, ft), weight_grad


def solution(mesh):
    return jax.shard_map(
        functools.partial(per_device, mesh.shape["lon"], mesh.shape["lat"]),
        mesh=mesh,
        in_specs=(
            P("lat", "lon", None),
            P(),
            P(None, "lat", "lon"),
            P(None, "lat", "lon"),
            P(None, "lat", "lon"),
            P(),
        ),
        out_specs=(P("lat", "lon", None), P("lon", None)),
        check_vma=False,
    )
```
